256 devices in a mesh: inst: 32 (over x_hi, z, core), tp: 8 (over y, x_lo).
Axes of the slice: x: 4 (x_hi: 2, x_lo: 2; x = x_hi * 2 + x_lo), y: 4, z: 8, core: 2. Of those that a mesh axis runs over, the one named last changes fastest.
Arguments:
- step_tokens: bfloat16 [4, 256, 2048], P(None, 'inst'), may hold values from -6 to 6
- delta_state: float32 [256, 16, 128, 128], P('inst', 'tp'), may hold values from -4 to 4
- kv_pages: bfloat16 [2048, 2, 64, 256], P('inst', None, 'tp'), may hold values from -240 to 240
- page_table: int32 [256, 8], P('inst'), may hold values from 0 to 63, as said below
- lengths: int32 [256], replicated, may hold values from 1 to 508
- moves: int32 [4, 16, 4], replicated, may hold values from 0 to 31, as said below
- delta_norm: bfloat16 [2048], replicated, may hold values from 0.25 to 1.75
- head_norm: bfloat16 [128], replicated, may hold values from 0.25 to 1.75
- w_qk: bfloat16 [2048, 2, 1024], P(None, None, 'tp'), may hold values from -0.125 to 0.125
- w_vz: bfloat16 [2048, 2, 2048], P(None, None, 'tp'), may hold values from -0.125 to 0.125
- w_ba: bfloat16 [2048, 2, 16], P(None, None, 'tp'), may hold values from -0.125 to 0.125
- a_log: float32 [16], P('tp'), may hold values from -2 to 1.5
- dt_bias: float32 [16], P('tp'), may hold values from -2 to 1
- w_out: bfloat16 [2048, 2048], P('tp'), may hold values from -0.125 to 0.125
- att_norm: bfloat16 [2048], replicated, may hold values from 0.25 to 1.75
- qk_norm: bfloat16 [2, 256], replicated, may hold values from 0.25 to 1.75
- w_q: bfloat16 [2048, 2048], P(None, 'tp'), may hold values from -0.125 to 0.125
- w_kv: bfloat16 [2048, 2, 256], replicated, may hold values from -0.125 to 0.125
- w_o: bfloat16 [2048, 2048], P('tp'), may hold values from -0.125 to 0.125
Outputs:
- mixed: bfloat16 [4, 256, 2048], P(None, 'inst')
- final_state: float32 [256, 16, 128, 128], P('inst', 'tp')
- final_pages: bfloat16 [2048, 2, 64, 256], P('inst', None, 'tp')
The draws below stay inside these ranges and needn't reach their ends.
Inputs may be any that keep to these rules, and one draw needn't show every extreme that they name: Each instance's rows of page_table hold each of 0 to 63 once. `moves`: within one step the 16 source instances and the 16 destination instances are 32 distinct instances; columns 1 and 3 are slots below 8.
All inputs are finite; a program needn't handle non-finite values.
Results may differ from the reference program's by a relative error of at most 0.04.
Values may be sent and summed in bfloat16 or wider, within the bound.
No kernel may reach another device: no remote copies, remote signals or barrier semaphores. Data moves between devices by JAX's collectives and lax.ppermute only.
A program may use at most 128 MiB of HBM per device.

```python
import jax
import jax.numpy as jnp
from jax import lax

D = 2048
HV = 16
HK = 8
DK = 128
DV = 128
QH = 8
HD = 256
B = 8
CTX = 512
PAGE = 64
STEPS = 4
PAGES_REQ = 8
POOL = 64
R = 256
PAIRS = 16
N_INST = 32


def draw_kv_pages(key, part):
    key = jax.random.fold_in(key, 14)
    base_key, scale_key = jax.random.split(key)
    shape = (N_INST * POOL, 2, PAGE, HD)
    base = jnp.clip(jax.random.normal(base_key, shape, jnp.float32), -6.0, 6.0)
    log_scale = jax.random.uniform(scale_key, (N_INST * POOL, 1, 1, 1), jnp.float32, 0.0, 3.6888795)
    page_scale = jnp.exp(log_scale)
    which = jnp.arange(2).reshape(1, 2, 1, 1)
    factor = jnp.where(which == 0, page_scale, 1.0)
    return (base * factor).astype(jnp.bfloat16)


def draw_page_table(key, part):
    key = jax.random.fold_in(key, 11)
    instance_keys = jax.random.split(key, N_INST)

    def one_pool(pool_key):
        return jax.random.permutation(pool_key, POOL)
    pools = jax.vmap(one_pool)(instance_keys)
    return pools.reshape(R, PAGES_REQ).astype(jnp.int32)


def draw_lengths(key, part):
    key = jax.random.fold_in(key, 12)
    first_key, second_key = jax.random.split(key)
    drawn = jax.random.randint(first_key, (R,), 1, CTX - STEPS + 1)
    longest = jax.random.randint(second_key, (), 0, R)
    return jnp.where(jnp.arange(R) == longest, CTX - STEPS, drawn).astype(jnp.int32)


def draw_moves(key, part):
    key = jax.random.fold_in(key, 13)
    step_keys = jax.random.split(key, STEPS)

    def one_step(step_key):
        order_key, source_key, target_key = jax.random.split(step_key, 3)
        order = jax.random.permutation(order_key, N_INST)
        source_slots = jax.random.randint(source_key, (PAIRS,), 0, B)
        target_slots = jax.random.randint(target_key, (PAIRS,), 0, B)
        return jnp.stack([order[:PAIRS], source_slots, order[PAIRS:2 * PAIRS], target_slots], axis=1)
    return jax.vmap(one_step)(step_keys).astype(jnp.int32)


def level_of(stream_key, shape, cuts, least, top_value):
    factor_of, own = 1.0, jax.random.fold_in(stream_key, 6)
    for axis_at, blocks in cuts:
        steps = jnp.exp(jax.random.uniform(jax.random.fold_in(own, axis_at), (blocks,), jnp.float32, least / len(cuts), top_value / len(cuts)))
        factor_of = factor_of * jnp.repeat(steps, shape[axis_at] // blocks).reshape([-1 if axis == axis_at else 1 for axis in range(len(shape))])
    return factor_of


def centred(own_key, extent, deviation, reach, shards=(), held_as=jnp.bfloat16):
    array = deviation * jax.random.normal(own_key, extent, jnp.float32)
    if shards:
        array = array * level_of(own_key, extent, shards, -0.22, 0.18)
    return jnp.clip(array, -reach, reach).astype(held_as)


def setup_inputs(seed: int = 0) -> dict:
    arg_keys = jax.random.split(jax.random.key(seed), 20)
    return {
        "step_tokens": centred(arg_keys[0], (STEPS, R, D), 1.0, 6.0, ((1, 32),)),
        "delta_state": centred(arg_keys[1], (R, HV, DK, DV), 0.5, 4.0, ((0, 32), (1, 8)), jnp.float32),
        "kv_pages": draw_kv_pages(jax.random.fold_in(arg_keys[19], 71), 0),
        "page_table": draw_page_table(jax.random.fold_in(arg_keys[19], 71), 0),
        "lengths": draw_lengths(jax.random.fold_in(arg_keys[19], 71), 0),
        "moves": draw_moves(jax.random.fold_in(arg_keys[19], 71), 0),
        "delta_norm": jnp.clip(1.0 + 0.15 * jax.random.normal(arg_keys[6], (D,), jnp.float32), 0.25, 1.75).astype(jnp.bfloat16),
        "head_norm": jnp.clip(1.0 + 0.15 * jax.random.normal(arg_keys[7], (DV,), jnp.float32), 0.25, 1.75).astype(jnp.bfloat16),
        "w_qk": centred(arg_keys[8], (D, 2, HK * DK), D ** -0.5, 0.125, ((2, 8),)),
        "w_vz": centred(arg_keys[9], (D, 2, HV * DV), D ** -0.5, 0.125, ((2, 8),)),
        "w_ba": centred(arg_keys[10], (D, 2, HV), D ** -0.5, 0.125, ((2, 8),)),
        "a_log": jnp.clip(-2.0 + 3.5 * jax.random.uniform(arg_keys[11], (HV,), jnp.float32) ** level_of(arg_keys[11], (HV,), ((0, 8),), -0.2, 0.2), -2.0, 1.5),
        "dt_bias": jnp.clip(-2.0 + 3.0 * jax.random.uniform(arg_keys[12], (HV,), jnp.float32) ** level_of(arg_keys[12], (HV,), ((0, 8),), -0.2, 0.2), -2.0, 1.0),
        "w_out": centred(arg_keys[13], (HV * DV, D), (HV * DV) ** -0.5, 0.125, ((0, 8),)),
        "att_norm": jnp.clip(1.0 + 0.15 * jax.random.normal(arg_keys[14], (D,), jnp.float32), 0.25, 1.75).astype(jnp.bfloat16),
        "qk_norm": jnp.clip(1.0 + 0.15 * jax.random.normal(arg_keys[15], (2, HD), jnp.float32), 0.25, 1.75).astype(jnp.bfloat16),
        "w_q": centred(arg_keys[16], (D, QH * HD), D ** -0.5, 0.125, ((1, 8),)),
        "w_kv": centred(arg_keys[17], (D, 2, HD), D ** -0.5, 0.125),
        "w_o": centred(arg_keys[18], (QH * HD, D), (QH * HD) ** -0.5, 0.125, ((0, 8),)),
    }


def rms_norm(values, gain_vec):
    scale = lax.rsqrt(lax.optimization_barrier(jnp.mean(values * values, axis=-1, keepdims=True)) + 1e-06)
    return values * scale * gain_vec.astype(jnp.float32)

def unit_heads(values):
    return values * lax.rsqrt(lax.optimization_barrier(jnp.sum(values * values, axis=-1, keepdims=True)) + 1e-06)

def to_float(values):
    return lax.optimization_barrier(values).astype(jnp.float32)

def migrate(states, kv_pool, context, page_table, pair_rows):
    source = pair_rows[:, 0] * B + pair_rows[:, 1]
    target = pair_rows[:, 2] * B + pair_rows[:, 3]
    states = states.at[target].set(states[source])
    states = states.at[source].set(jnp.zeros_like(states[source]))
    source_pages = (page_table[source] + pair_rows[:, 0:1] * POOL).reshape(-1)
    target_pages = (page_table[target] + pair_rows[:, 2:3] * POOL).reshape(-1)
    kv_pool = kv_pool.at[target_pages].set(kv_pool[source_pages])
    context = context.at[target].set(context[source])
    context = context.at[source].set(jnp.zeros_like(context[source]))
    return (states, kv_pool, context)

def delta_layer(hidden, states, delta_norm, head_norm, w_qk, w_vz, w_ba, a_log, dt_bias, w_out):
    row_count = hidden.shape[0]
    normed = to_float(rms_norm(hidden, delta_norm).astype(jnp.bfloat16))
    pair_qk = jnp.einsum('bd,dtc->btc', normed, w_qk.astype(jnp.float32))
    pair_vz = jnp.einsum('bd,dtc->btc', normed, w_vz.astype(jnp.float32))
    pair_ba = jnp.einsum('bd,dtc->btc', normed, w_ba.astype(jnp.float32))
    group_size = HV // HK
    queries = jnp.repeat(unit_heads(pair_qk[:, 0].reshape(row_count, HK, DK)), group_size, axis=1) * DK ** (-0.5)
    key_dirs = jnp.repeat(unit_heads(pair_qk[:, 1].reshape(row_count, HK, DK)), group_size, axis=1)
    values = pair_vz[:, 0].reshape(row_count, HV, DV)
    gate_z = pair_vz[:, 1].reshape(row_count, HV, DV)
    write_rate = jax.nn.sigmoid(pair_ba[:, 0])
    decays = jnp.exp(-jnp.exp(a_log.astype(jnp.float32)) * jax.nn.softplus(pair_ba[:, 1] + dt_bias.astype(jnp.float32)))
    states = states * decays[:, :, None, None]
    recalled = jnp.einsum('bhk,bhkv->bhv', key_dirs, states, precision=lax.Precision.HIGHEST)
    update = write_rate[:, :, None] * (values - recalled)
    states = states + key_dirs[:, :, :, None] * update[:, :, None, :]
    readout = jnp.einsum('bhk,bhkv->bhv', queries, states, precision=lax.Precision.HIGHEST)
    readout = rms_norm(readout, head_norm) * jax.nn.silu(gate_z)
    readout = readout.astype(jnp.bfloat16).reshape(row_count, HV * DV)
    return (hidden + jnp.dot(readout, w_out, preferred_element_type=jnp.float32), states)

def attend(hidden, kv_pool, context, page_table, att_norm, qk_norm, w_q, w_kv, w_o):
    row_count = hidden.shape[0]
    normed_bf = rms_norm(hidden, att_norm).astype(jnp.bfloat16)
    queries = jnp.dot(normed_bf, w_q, preferred_element_type=jnp.float32).reshape(row_count, QH, HD)
    queries = rms_norm(queries, qk_norm[0]).astype(jnp.bfloat16)
    kv_new = jnp.einsum('bd,dtc->btc', to_float(normed_bf), w_kv.astype(jnp.float32))
    new_entry = jnp.stack([rms_norm(kv_new[:, 0], qk_norm[1]), kv_new[:, 1]], axis=1).astype(jnp.bfloat16)
    owner_inst = (jnp.arange(row_count) // B).astype(jnp.int32)
    slot_ids = jnp.arange(row_count)
    page_of = page_table[slot_ids, context // PAGE] + owner_inst * POOL
    kv_pool = kv_pool.at[page_of, :, context % PAGE, :].set(new_entry)
    pages_all = page_table + owner_inst[:, None] * POOL

    def attend_slot(slot_args):
        query_one, pages_one, length_one = slot_args
        context_kv = kv_pool[pages_one]
        key_rows = context_kv[:, 0].reshape(CTX, HD)
        value_rows = context_kv[:, 1].reshape(CTX, HD)
        scores = jnp.dot(query_one, key_rows.T, preferred_element_type=jnp.float32) / math_sqrt_hd()
        visible = jnp.arange(CTX) <= length_one
        scores = jnp.where(visible[None, :], scores, -1e+30)
        highest = lax.optimization_barrier(jnp.max(scores, axis=-1, keepdims=True))
        weights = jnp.where(visible[None, :], jnp.exp(scores - highest), 0.0)
        weight_sum = lax.optimization_barrier(jnp.sum(weights, axis=-1, keepdims=True))
        head_out = jnp.dot(weights.astype(jnp.bfloat16), value_rows, preferred_element_type=jnp.float32) / weight_sum
        return head_out.astype(jnp.bfloat16)
    head_out = lax.map(attend_slot, (queries, pages_all, context))
    projected = jnp.dot(head_out.reshape(row_count, QH * HD), w_o, preferred_element_type=jnp.float32)
    return (hidden + projected, kv_pool)

def math_sqrt_hd():
    return float(HD) ** 0.5

def reference(step_tokens, delta_state, kv_pages, page_table, lengths, moves, delta_norm, head_norm, w_qk, w_vz, w_ba, a_log, dt_bias, w_out, att_norm, qk_norm, w_q, w_kv, w_o):
    states = delta_state
    kv_pool = kv_pages
    context = lengths
    outputs = []
    for step_index in range(STEPS):
        states, kv_pool, context = migrate(states, kv_pool, context, page_table, moves[step_index])
        hidden = step_tokens[step_index].astype(jnp.float32)
        hidden, states = delta_layer(hidden, states, delta_norm, head_norm, w_qk, w_vz, w_ba, a_log, dt_bias, w_out)
        hidden, kv_pool = attend(hidden, kv_pool, context, page_table, att_norm, qk_norm, w_q, w_kv, w_o)
        outputs.append(hidden.astype(jnp.bfloat16))
        context = context + 1
    return (jnp.stack(outputs), states, kv_pool)
```

```python
import jax
import jax.numpy as jnp
from jax import lax
from jax.experimental import pallas as pl
from jax.experimental.pallas import tpu as pltpu
from jax.sharding import PartitionSpec as P

F32 = jnp.float32
BF16 = jnp.bfloat16
STEPS = 4
SLOTS = 8
INSTS = 32
PARTS = 8
OWN = 32
ROWS = 48
DK = 128
HD = 256
D = 2048

I_LEN = 256
I_TAB = 512
I_ME = 576

T_SLOT = 0
T_FROM = 128
T_ITEM = 256
T_TOK = 384
T_OWN = 640
T_IN = 644
T_NEW = 648
T_RLEN = 656
T_OLEN = 664
T_SIZE = 768

FIRST = (0, 0, 1, 3)

SMEM = pl.BlockSpec(memory_space=pltpu.SMEM)
VMEM = pl.BlockSpec(memory_space=pltpu.VMEM)
PARAMS = pltpu.CompilerParams(vmem_limit_bytes=48 * 1024 * 1024)


def call(kernel, ins, outs, scratch=(), out_specs=None):
    return pl.pallas_call(
        kernel,
        in_specs=list(ins),
        out_specs=[VMEM] * len(outs) if out_specs is None else out_specs,
        out_shape=list(outs),
        scratch_shapes=list(scratch),
        compiler_params=PARAMS,
    )


def rms(values, gain):
    return values * lax.rsqrt(jnp.mean(values * values, axis=-1, keepdims=True) + 1e-06) * gain


def unit(values):
    return values * lax.rsqrt(jnp.sum(values * values, axis=-1, keepdims=True) + 1e-06)


def pack_kernel(ints, state, pages, tokens, out, tab, tok_scr, row_scr):
    def note(i, carry):
        s = lax.shift_right_logical(i, 4)
        a, c, e, f = (ints[i * 4 + n] for n in range(4))
        source, target = a * SLOTS + c, e * SLOTS + f
        tab[T_SLOT + s * INSTS + a] = source
        tab[T_FROM + s * INSTS + a] = -1
        tab[T_SLOT + s * INSTS + e] = target
        tab[T_FROM + s * INSTS + e] = source
        return carry

    lax.fori_loop(0, 64, note, 0)
    me = ints[I_ME]

    def trace(e, s, at_row):
        cur = jnp.maximum(tab[T_FROM + s * INSTS + e], 0)
        hop = jnp.int32(s)
        fresh = {}
        for t in range(s - 1, -1, -1):
            h = lax.shift_right_logical(cur, 3)
            at_row(t, h, hop)
            slot, origin = tab[T_SLOT + t * INSTS + h], tab[T_FROM + t * INSTS + h]
            hit = slot == cur
            fresh[t] = jnp.logical_and(hit, origin < 0)
            moved = jnp.logical_and(hit, origin >= 0)
            cur = jnp.where(moved, origin, cur)
            hop = jnp.where(moved, t, hop)
        return cur, hop, fresh

    def route(e, carry):
        tab[T_TOK + e * 8 + 6] = 0
        tab[T_TOK + e * 8 + 7] = 0
        for s in range(STEPS):

            def at_row(t, h, hop, s=s):
                first = lax.shift_right_logical(hop * (hop - 1), 1)
                tab[T_TOK + e * 8 + FIRST[s] + t] = h * 8 + first + t

            cur, hop, _ = trace(e, s, at_row)
            tab[T_ITEM + e * 4 + s] = lax.shift_right_logical(cur, 3) * 5 + hop
        return carry

    lax.fori_loop(0, INSTS, route, 0)

    held = [ints[I_LEN + me * SLOTS + b] for b in range(SLOTS)]
    for s in range(STEPS):
        slot = tab[T_SLOT + s * INSTS + me] & 7
        moved_in = tab[T_FROM + s * INSTS + me] >= 0
        tab[T_OWN + s] = slot
        tab[T_IN + s] = moved_in.astype(jnp.int32)
        root, _, fresh = trace(me, s, lambda t, h, hop: None)
        length = ints[I_LEN + root]
        for t in range(s):
            length = jnp.where(fresh[t], -t, length)
            tab[T_NEW + FIRST[s] + t] = fresh[t].astype(jnp.int32)
            tab[T_RLEN + FIRST[s] + t] = length + t
        arriving = jnp.where(moved_in, length, -s)
        for b in range(SLOTS):
            held[b] = jnp.where(slot == b, arriving, held[b])
            tab[T_OLEN + s * SLOTS + b] = held[b] + s

    for s in range(STEPS):
        tok_scr[s * 8 : s * 8 + 8, :] = tokens[s].astype(F32)
    row_scr[...] = jnp.zeros_like(row_scr)
    for s in range(STEPS):
        slot = tab[T_OWN + s]
        for t in range(s):
            row_scr[FIRST[s] + t : FIRST[s] + t + 1, :] = tok_scr[pl.ds(t * 8 + slot, 1), :]
    for s in range(STEPS):
        slot = tab[T_OWN + s]
        for i in range(INSTS):
            page = ints[I_TAB + slot * 8 + i // 4]
            half = (i % 2) * 128
            a = state[slot, i // 16, (i % 16) * 8 : (i % 16) * 8 + 8, :]
            b = pages[page, (i // 2) % 2, :, half : half + 128].astype(F32)
            out[i, s] = jnp.concatenate([a, b], axis=0).astype(BF16)
    blank = jnp.zeros((8, 128), F32)
    for i in range(INSTS):
        a = row_scr[:, i * 128 : i * 128 + 128] if i < 16 else blank
        out[i, 4] = jnp.concatenate([a, blank], axis=0).astype(BF16)


def select_kernel(tab, got, out, in_scr, out_scr):
    for h in range(INSTS):
        in_scr[h * 8 : h * 8 + 8, :] = got[h * 5 + 4].astype(F32)[:8]
    out_scr[...] = jnp.zeros_like(out_scr)

    def pick(e, carry):
        for s in range(STEPS):
            out[e * 5 + s] = got[tab[T_ITEM + e * 4 + s]]
        for r in range(6):
            out_scr[pl.ds(e * 16 + r, 1), :] = in_scr[pl.ds(tab[T_TOK + e * 8 + r], 1), :]
        return carry

    lax.fori_loop(0, INSTS, pick, 0)
    for e in range(INSTS):
        out[e * 5 + 4] = out_scr[e * 16 : e * 16 + 16, :].astype(BF16)


def norm_kernel(tokens, got, gain, out, scr):
    for s in range(STEPS):
        scr[s * 8 : s * 8 + 8, :] = tokens[s].astype(F32)
    for i in range(16):
        scr[32:48, i * 128 : i * 128 + 128] = got[i, 4].astype(F32)
    out[...] = rms(scr[...], gain[...].astype(F32)).astype(BF16)


def delta_kernel(tab, qk, vz, ba, a_log, dt_bias, head_gain, w_out, state, got, out, final, o_scr):
    q = unit(qk[0]) * DK ** (-0.5)
    k = unit(qk[1])
    kq = jnp.broadcast_to(jnp.sum(k * q, axis=-1, keepdims=True), (ROWS, 128))
    q_cols, k_cols = q.T, k.T
    rate = jax.nn.sigmoid(ba[0])
    x = ba[1] + dt_bias[...]
    softplus = jnp.maximum(x, 0.0) + jnp.log1p(jnp.exp(-jnp.abs(x)))
    decay = jnp.exp(-jnp.exp(a_log[...]) * softplus)
    rates = [jnp.broadcast_to(rate[:, m : m + 1], (ROWS, 128)) for m in range(2)]
    decays = [jnp.broadcast_to(decay[:, m : m + 1], (ROWS, 128)) for m in range(2)]
    values = [vz[0, :, m * 128 : m * 128 + 128] for m in range(2)]

    def update(held, row, m):
        at = slice(row, row + 1)
        k_col, q_col = k_cols[:, at], q_cols[:, at]
        d = decays[m][at]
        u = rates[m][at] * (values[m][at] - d * jnp.sum(held * k_col, axis=0, keepdims=True))
        o = d * jnp.sum(held * q_col, axis=0, keepdims=True) + kq[at] * u
        o_scr[at, m * 128 : m * 128 + 128] = o
        return held * d + k_col * u

    o_scr[...] = jnp.zeros_like(o_scr)
    final[...] = state[...]
    for s in range(STEPS):
        slot = tab[T_OWN + s]

        @pl.when(tab[T_IN + s] == 0)
        def _():
            final[slot] = jnp.zeros((2, 128, 128), F32)

        @pl.when(tab[T_IN + s] == 1)
        def _():
            for m in range(2):
                held = jnp.concatenate(
                    [got[m * 16 + i, s].astype(F32)[:8] for i in range(16)], axis=0
                )
                for t in range(s):
                    r = FIRST[s] + t
                    held = jnp.where(tab[T_NEW + r] == 1, 0.0, held)
                    held = update(held, OWN + r, m)
                final[slot, m] = held

        for b in range(SLOTS):
            for m in range(2):
                final[b, m] = update(final[b, m], s * SLOTS + b, m)

    y = [
        rms(o_scr[:, m * 128 : m * 128 + 128], head_gain[...].astype(F32))
        * jax.nn.silu(vz[1, :, m * 128 : m * 128 + 128])
        for m in range(2)
    ]
    y = jnp.concatenate(y, axis=1).astype(BF16)
    part = jnp.dot(y, w_out[...], preferred_element_type=F32).astype(BF16)
    for n in range(PARTS):
        out[n] = part


def hidden_kernel(rows, got, gain, w_q, q_gain, hidden, normed, query):
    total = rows[...]
    for n in range(PARTS):
        total = total + got[n].astype(F32)
    hidden[...] = total[:OWN]
    n2 = rms(total, gain[...].astype(F32)).astype(BF16)
    normed[...] = n2
    q = jnp.dot(n2[:OWN], w_q[...], preferred_element_type=F32)
    q = rms(q, q_gain[0:1, :].astype(F32)).astype(BF16)
    for n in range(PARTS):
        query[n] = q


def pages_kernel(ints, tab, pages, got, query, kv, kv_gain, out, final, key, val, new, q_scr, o_scr):
    part = ints[I_ME + 1]
    new[0] = rms(kv[0], kv_gain[1:2, :].astype(F32)).astype(BF16).astype(F32)
    new[1] = kv[1].astype(BF16).astype(F32)
    q_scr[...] = query[...].astype(F32)
    for i in range(64):
        page = ints[I_TAB + i]
        key[i] = pages[page, 0].astype(F32)
        val[i] = pages[page, 1].astype(F32)

    def write(slot, length, row):
        offset = length & 63
        block = slot * 8 + lax.shift_right_logical(length, 6)

        @pl.when(lax.shift_right_logical(offset, 3) == part)
        def _():
            at = pl.ds(offset & 7, 1)
            key[block, at, :] = new[0, row : row + 1, :]
            val[block, at, :] = new[1, row : row + 1, :]

    column = lax.broadcasted_iota(jnp.int32, (1, 512), 1)
    column_slot = lax.shift_right_logical(column, 6)
    position = (lax.shift_right_logical(column, 3) & 7) * 64 + part * 8 + (column & 7)
    row_slot = lax.broadcasted_iota(jnp.int32, (64, 512), 0) & 7
    same = row_slot == lax.broadcasted_iota(jnp.int32, (64, 512), 1) // 64
    lane = lax.broadcasted_iota(jnp.int32, (64, 128), 1)
    for s in range(STEPS):
        slot = tab[T_OWN + s]

        @pl.when(tab[T_IN + s] == 1)
        def _():
            for i in range(INSTS):
                half = (i % 2) * 128
                rows = got[i, s].astype(F32)[8:]
                to = key if (i // 2) % 2 == 0 else val
                to[slot * 8 + i // 4, :, half : half + 128] = rows
            for t in range(s):
                write(slot, tab[T_RLEN + FIRST[s] + t], OWN + FIRST[s] + t)

        lengths = jnp.zeros((1, 512), jnp.int32)
        for b in range(SLOTS):
            length = tab[T_OLEN + s * SLOTS + b]
            write(b, length, s * SLOTS + b)
            lengths = jnp.where(column_slot == b, length, lengths)
        visible = jnp.logical_and(same, position <= lengths)
        q = q_scr[:, s * 8 : s * 8 + 8, :].reshape(64, HD).astype(BF16)
        k = key[...].reshape(512, HD).astype(BF16)
        v = val[...].reshape(512, HD).astype(BF16)
        scores = lax.dot_general(
            q, k, (((1,), (1,)), ((), ())), preferred_element_type=F32
        ) * (float(HD) ** -0.5)
        scores = jnp.where(visible, scores, -1e30)
        top = jnp.max(scores, axis=-1, keepdims=True).astype(BF16).astype(F32)
        weights = jnp.where(visible, jnp.exp(scores - top), 0.0)
        total = jnp.sum(weights, axis=-1, keepdims=True)
        high = total.astype(BF16).astype(F32)
        low = total - high
        mixed = jnp.dot(weights.astype(BF16), v, preferred_element_type=F32)
        stats = jnp.where(lane == 0, top, jnp.where(lane == 1, high, jnp.where(lane == 2, low, 0.0)))
        mixed = jnp.concatenate([mixed, stats], axis=1)
        o_scr[:, s * 8 : s * 8 + 8, :] = mixed.reshape(PARTS, 8, 384)
    out[...] = o_scr[...].astype(BF16)
    for i in range(64):
        page = ints[I_TAB + i]
        final[page, 0] = key[i].astype(BF16)
        final[page, 1] = val[i].astype(BF16)


def merge_kernel(got, w_o, out):
    shares = [got[n].astype(F32) for n in range(PARTS)]
    tops = [x[:, 256:257] for x in shares]
    top = tops[0]
    for x in tops[1:]:
        top = jnp.maximum(top, x)
    total = jnp.zeros((OWN, 1), F32)
    mixed = jnp.zeros((OWN, HD), F32)
    for x, own in zip(shares, tops, strict=True):
        scale = jnp.exp(own - top)
        total = total + (x[:, 257:258] + x[:, 258:259]) * scale
        mixed = mixed + x[:, :256] * scale
    head = (mixed / total).astype(BF16)
    part = jnp.dot(head, w_o[...], preferred_element_type=F32).astype(BF16)
    for n in range(PARTS):
        out[n] = part


def last_kernel(hidden, got, out):
    total = hidden[...]
    for n in range(PARTS):
        total = total + got[n].astype(F32)
    for s in range(STEPS):
        out[s] = total[s * 8 : s * 8 + 8].astype(BF16)


def body(
    step_tokens,
    delta_state,
    kv_pages,
    page_table,
    lengths,
    moves,
    delta_norm,
    head_norm,
    w_qk,
    w_vz,
    w_ba,
    a_log,
    dt_bias,
    w_out,
    att_norm,
    qk_norm,
    w_q,
    w_kv,
    w_o,
):
    shape = jax.ShapeDtypeStruct
    me = jnp.stack([lax.axis_index("inst"), lax.axis_index("tp")]).astype(jnp.int32)
    ints = jnp.concatenate([moves.reshape(-1), lengths, page_table.reshape(-1), me])

    packed, tab = call(
        pack_kernel,
        [SMEM, VMEM, VMEM, VMEM],
        [shape((INSTS, 5, 16, 128), BF16), shape((T_SIZE,), jnp.int32)],
        [pltpu.VMEM((OWN, D), F32), pltpu.VMEM((8, D), F32)],
        [VMEM, SMEM],
    )(ints, delta_state, kv_pages, step_tokens)
    got = lax.all_to_all(packed.reshape(INSTS, 80, 128), "inst", 0, 0)
    (picked,) = call(
        select_kernel,
        [SMEM, VMEM],
        [shape((INSTS * 5, 16, 128), BF16)],
        [pltpu.VMEM((INSTS * 8, 128), F32), pltpu.VMEM((INSTS * 16, 128), F32)],
    )(tab, got.reshape(INSTS * 5, 16, 128))
    got = lax.all_to_all(picked.reshape(INSTS, 80, 128), "inst", 0, 0)
    got = got.reshape(INSTS, 5, 16, 128)

    n1, rows = call(
        norm_kernel,
        [VMEM] * 3,
        [shape((ROWS, D), BF16), shape((ROWS, D), F32)],
    )(step_tokens, got, delta_norm.reshape(1, D))
    qk = jnp.einsum("bd,dtc->tbc", n1, w_qk, preferred_element_type=F32)
    vz = jnp.einsum("bd,dtc->tbc", n1, w_vz, preferred_element_type=F32)
    ba = jnp.einsum("bd,dtc->tbc", n1, w_ba, preferred_element_type=F32)
    part, final_state = call(
        delta_kernel,
        [SMEM] + [VMEM] * 9,
        [shape((PARTS, ROWS, D), BF16), shape(delta_state.shape, F32)],
        [pltpu.VMEM((ROWS, 256), F32)],
    )(
        tab,
        qk,
        vz,
        ba,
        a_log.reshape(1, 2),
        dt_bias.reshape(1, 2),
        head_norm.reshape(1, 128),
        w_out,
        delta_state,
        got,
    )
    parts = lax.all_to_all(part, "tp", 0, 0)
    hidden, n2, query = call(
        hidden_kernel,
        [VMEM] * 5,
        [shape((OWN, D), F32), shape((ROWS, D), BF16), shape((PARTS, OWN, HD), BF16)],
    )(rows, parts, att_norm.reshape(1, D), w_q, qk_norm)
    queries = lax.all_to_all(query, "tp", 0, 0)
    kv = jnp.einsum("bd,dtc->tbc", n2, w_kv, preferred_element_type=F32)
    shares, final_pages = call(
        pages_kernel,
        [SMEM, SMEM] + [VMEM] * 5,
        [shape((PARTS, OWN, 384), BF16), shape(kv_pages.shape, BF16)],
        [
            pltpu.VMEM((64, 8, HD), F32),
            pltpu.VMEM((64, 8, HD), F32),
            pltpu.VMEM((2, ROWS, HD), F32),
            pltpu.VMEM((PARTS, OWN, HD), F32),
            pltpu.VMEM((PARTS, OWN, 384), F32),
        ],
    )(ints, tab, kv_pages, got, queries, kv, qk_norm)
    shares = lax.all_to_all(shares, "tp", 0, 0)
    (part,) = call(merge_kernel, [VMEM] * 2, [shape((PARTS, OWN, D), BF16)])(shares, w_o)
    parts = lax.all_to_all(part, "tp", 0, 0)
    (mixed,) = call(last_kernel, [VMEM] * 2, [shape(step_tokens.shape, BF16)])(hidden, parts)
    return (mixed, final_state, final_pages)


def solution(mesh):
    in_specs = (
        P(None, "inst", None),
        P("inst", "tp", None, None),
        P("inst", None, "tp", None),
        P("inst", None),
        P(),
        P(),
        P(),
        P(),
        P(None, None, "tp"),
        P(None, None, "tp"),
        P(None, None, "tp"),
        P("tp"),
        P("tp"),
        P("tp", None),
        P(),
        P(),
        P(None, "tp"),
        P(),
        P("tp", None),
    )
    out_specs = (P(None, "inst", None), P("inst", "tp", None, None), P("inst", None, "tp", None))
    return jax.shard_map(body, mesh=mesh, in_specs=in_specs, out_specs=out_specs, check_vma=False)
```

```python
import jax
import jax.numpy as jnp
from jax import lax
from jax.experimental import pallas as pl
from jax.experimental.pallas import tpu as pltpu
from jax.sharding import PartitionSpec as P

F32 = jnp.float32
BF16 = jnp.bfloat16
STEPS = 4
SLOTS = 8
INSTS = 32
PARTS = 8
OWN = 32
ROWS = 48
EXTRA = 16
PIECE = 72
DK = 128
HD = 256
D = 2048

T_SLOT = 0
T_FROM = 128
T_ITEM = 256
T_TOK = 384
T_OWN = 640
T_IN = 644
T_NEW = 648
T_RLEN = 656
T_OLEN = 664
T_SIZE = 768

FIRST = (0, 0, 1, 3)
LATE = (6, 10, 13, 15)

SMEM = pl.BlockSpec(memory_space=pltpu.SMEM)
VMEM = pl.BlockSpec(memory_space=pltpu.VMEM)
HBM = pl.BlockSpec(memory_space=pltpu.HBM)
ANY = pl.BlockSpec(memory_space=pl.ANY)
PARAMS = pltpu.CompilerParams(vmem_limit_bytes=48 * 1024 * 1024)


def call(kernel, ins, outs, scratch=(), out_specs=None):
    return pl.pallas_call(
        kernel,
        in_specs=list(ins),
        out_specs=[VMEM] * len(outs) if out_specs is None else out_specs,
        out_shape=list(outs),
        scratch_shapes=list(scratch),
        compiler_params=PARAMS,
    )


def rms(values, gain):
    return values * lax.rsqrt(jnp.mean(values * values, axis=-1, keepdims=True) + 1e-06) * gain


def unit(values):
    return values * lax.rsqrt(jnp.sum(values * values, axis=-1, keepdims=True) + 1e-06)


def own_slots(moves, me):
    slots = []
    for s in range(STEPS):
        slot = jnp.int32(0)
        for p in range(16):
            slot = jnp.where(moves[s, 0, p] == me, moves[s, 1, p], slot)
            slot = jnp.where(moves[s, 2, p] == me, moves[s, 3, p], slot)
        slots.append(slot)
    return slots


def pack_kernel(
    moves, place, table, state, pages, tokens, out, st_scr, pg_scr, bf_scr, tok_scr, row_scr, sem
):
    slots = own_slots(moves, place[0])
    token_copy = pltpu.make_async_copy(tokens, bf_scr, sem.at[36])
    token_copy.start()
    copies = []
    for s in range(STEPS):
        copies.append(pltpu.make_async_copy(state.at[slots[s]], st_scr.at[s], sem.at[32 + s]))
        for j in range(8):
            at = s * 8 + j
            copies.append(
                pltpu.make_async_copy(pages.at[table[slots[s], j]], pg_scr.at[at], sem.at[at])
            )
    for copy in copies:
        copy.start()
    token_copy.wait()
    for s in range(STEPS):
        tok_scr[s * 8 : s * 8 + 8, :] = bf_scr[s].astype(F32)
    row_scr[...] = jnp.zeros_like(row_scr)
    for s in range(STEPS):
        for t in range(s):
            row_scr[FIRST[s] + t : FIRST[s] + t + 1, :] = tok_scr[pl.ds(t * 8 + slots[s], 1), :]
    for copy in copies:
        copy.wait()
    blank = jnp.zeros((8, 128), F32)
    for i in range(INSTS):
        at, half = (i % 16) * 8, (i % 2) * 128
        tiles = [st_scr[s, i // 16, at : at + 8, :] for s in range(STEPS)]
        for s in range(STEPS):
            page = pg_scr[s * 8 + i // 4, (i // 2) % 2].astype(F32)
            tiles.append(page[:, half : half + 128])
        tiles.append(row_scr[:, i * 128 : i * 128 + 128] if i < 16 else blank)
        out[i] = jnp.concatenate(tiles, axis=0).astype(BF16)


def table_kernel(moves, place, lens, tab):
    for s in range(STEPS):
        for p in range(16):
            a, c, e, f = (moves[s, n, p] for n in range(4))
            source, target = a * SLOTS + c, e * SLOTS + f
            tab[T_SLOT + s * INSTS + a] = source
            tab[T_FROM + s * INSTS + a] = -1
            tab[T_SLOT + s * INSTS + e] = target
            tab[T_FROM + s * INSTS + e] = source
    me = place[0]

    def trace(e, s, at_row):
        cur = jnp.maximum(tab[T_FROM + s * INSTS + e], 0)
        hop = jnp.int32(s)
        fresh = {}
        for t in range(s - 1, -1, -1):
            h = lax.shift_right_logical(cur, 3)
            at_row(t, h, hop)
            slot, origin = tab[T_SLOT + t * INSTS + h], tab[T_FROM + t * INSTS + h]
            hit = slot == cur
            fresh[t] = jnp.logical_and(hit, origin < 0)
            moved = jnp.logical_and(hit, origin >= 0)
            cur = jnp.where(moved, origin, cur)
            hop = jnp.where(moved, t, hop)
        return cur, hop, fresh

    def route(e, carry):
        for s in range(STEPS):

            def at_row(t, h, hop, s=s):
                first = lax.shift_right_logical(hop * (hop - 1), 1)
                tab[T_TOK + e * 8 + FIRST[s] + t] = h * PIECE + 64 + first + t

            cur, hop, _ = trace(e, s, at_row)
            tab[T_ITEM + e * 4 + s] = lax.shift_right_logical(cur, 3) * PIECE + hop * 8
        return carry

    lax.fori_loop(0, INSTS, route, 0)

    held = [lens[me * SLOTS + b] for b in range(SLOTS)]
    for s in range(STEPS):
        slot = tab[T_SLOT + s * INSTS + me] & 7
        moved_in = tab[T_FROM + s * INSTS + me] >= 0
        tab[T_OWN + s] = slot
        tab[T_IN + s] = moved_in.astype(jnp.int32)
        root, _, fresh = trace(me, s, lambda t, h, hop: None)
        length = lens[root]
        for t in range(s):
            length = jnp.where(fresh[t], -t, length)
            tab[T_NEW + FIRST[s] + t] = fresh[t].astype(jnp.int32)
            tab[T_RLEN + FIRST[s] + t] = length + t
        arriving = jnp.where(moved_in, length, -s)
        for b in range(SLOTS):
            held[b] = jnp.where(slot == b, arriving, held[b])
            tab[T_OLEN + s * SLOTS + b] = held[b] + s


def select_kernel(tab, got, early, out, in_scr, out_scr):
    for h in range(INSTS):
        in_scr[h * PIECE : (h + 1) * PIECE, :] = got[h].astype(F32)
    for e in range(INSTS):
        out_scr[e * PIECE + 64 : (e + 1) * PIECE, :] = jnp.zeros((8, 128), F32)

    def pick(e, carry):
        base = e * PIECE
        for s in range(STEPS):
            item = tab[T_ITEM + e * 4 + s]
            for n in (0, 32):
                at = pl.ds(pl.multiple_of(item + n, 8), 8)
                to = pl.ds(pl.multiple_of(base + (s * 8 + n), 8), 8)
                out_scr[to, :] = in_scr[at, :]
        for r in range(6):
            out_scr[pl.ds(base + (64 + r), 1), :] = in_scr[pl.ds(tab[T_TOK + e * 8 + r], 1), :]
        return carry

    lax.fori_loop(0, INSTS, pick, 0, unroll=4)
    for e in range(INSTS):
        out[e] = out_scr[e * PIECE : (e + 1) * PIECE, :].astype(BF16)


def norm_kernel(tokens, gain, out, scr):
    for s in range(STEPS):
        scr[s * 8 : s * 8 + 8, :] = tokens[s].astype(F32)
    out[...] = rms(scr[...], gain[...].astype(F32)).astype(BF16)


def late_norm_kernel(got, gain, out, rows):
    rows[...] = jnp.zeros_like(rows)
    for i in range(16):
        rows[0:8, i * 128 : i * 128 + 128] = got[i].astype(F32)[64:]
    out[...] = rms(rows[...], gain[...].astype(F32)).astype(BF16)


def updater(qk, vz, ba, a_log, dt_bias, o_scr):
    rows = qk.shape[1]
    q = unit(qk[0]) * DK ** (-0.5)
    k = unit(qk[1])
    kq = jnp.broadcast_to(jnp.sum(k * q, axis=-1, keepdims=True), (rows, 128))
    q_cols, k_cols = q.T, k.T
    rate = jax.nn.sigmoid(ba[0])
    x = ba[1] + dt_bias[...]
    softplus = jnp.maximum(x, 0.0) + jnp.log1p(jnp.exp(-jnp.abs(x)))
    decay = jnp.exp(-jnp.exp(a_log[...]) * softplus)
    rates = [jnp.broadcast_to(rate[:, m : m + 1], (rows, 128)) for m in range(2)]
    decays = [jnp.broadcast_to(decay[:, m : m + 1], (rows, 128)) for m in range(2)]
    values = [vz[0, :, m * 128 : m * 128 + 128] for m in range(2)]

    def update(held, row, m):
        at = slice(row, row + 1)
        k_col, q_col = k_cols[:, at], q_cols[:, at]
        d = decays[m][at]
        u = rates[m][at] * (values[m][at] - d * jnp.sum(held * k_col, axis=0, keepdims=True))
        o = d * jnp.sum(held * q_col, axis=0, keepdims=True) + kq[at] * u
        o_scr[at, m * 128 : m * 128 + 128] = o
        return held * d + k_col * u

    return update


def gated(o_scr, z, gain, w_out):
    y = [
        rms(o_scr[:, m * 128 : m * 128 + 128], gain[...].astype(F32))
        * jax.nn.silu(z[:, m * 128 : m * 128 + 128])
        for m in range(2)
    ]
    y = jnp.concatenate(y, axis=1).astype(BF16)
    return jnp.dot(y, w_out[...], preferred_element_type=F32).astype(BF16)


def early_kernel(tab, qk, vz, ba, a_log, dt_bias, head_gain, w_out, state, out, final, o_scr):
    update = updater(qk, vz, ba, a_log, dt_bias, o_scr)
    final[...] = state[...]
    for s in range(STEPS):
        slot = tab[T_OWN + s]

        @pl.when(tab[T_IN + s] == 0)
        def _():
            final[slot] = jnp.zeros((2, 128, 128), F32)

        for b in range(SLOTS):
            for m in range(2):
                final[b, m] = update(final[b, m], s * SLOTS + b, m)
    out[...] = gated(o_scr, vz[1], head_gain, w_out)


def late_kernel(
    tab,
    qk,
    vz,
    ba,
    qk_in,
    vz_in,
    ba_in,
    a_log,
    dt_bias,
    head_gain,
    w_out,
    got,
    out,
    states,
    qk_scr,
    vz_scr,
    ba_scr,
    o_scr,
):
    for scr, new, old in ((qk_scr, qk_in, qk), (vz_scr, vz_in, vz), (ba_scr, ba_in, ba)):
        for n in range(2):
            scr[n, 0:8, :] = new[n, 0:8, :]
            for s in range(STEPS):
                for t in range(s, STEPS):
                    row = LATE[s] + t - s
                    scr[n, row : row + 1, :] = old[n, pl.ds(t * 8 + tab[T_OWN + s], 1), :]
    update = updater(qk_scr, vz_scr, ba_scr, a_log, dt_bias, o_scr)
    o_scr[...] = jnp.zeros_like(o_scr)
    for s in range(STEPS):
        slot = tab[T_OWN + s]

        @pl.when(tab[T_IN + s] == 1)
        def _():
            for m in range(2):
                held = jnp.concatenate(
                    [got[m * 16 + i].astype(F32)[s * 8 : s * 8 + 8] for i in range(16)], axis=0
                )
                for t in range(s):
                    r = FIRST[s] + t
                    held = jnp.where(tab[T_NEW + r] == 1, 0.0, held)
                    held = update(held, r, m)
                for t in range(s, STEPS):
                    if t > s:
                        leaves = jnp.logical_and(tab[T_OWN + t] == slot, tab[T_IN + t] == 0)
                        held = jnp.where(leaves, 0.0, held)
                    held = update(held, LATE[s] + t - s, m)
                states[s, m] = held

    part = gated(o_scr, vz_scr[1], head_gain, w_out)
    for n in range(PARTS):
        out[n] = part


def states_kernel(tab, early, late, final):
    final[...] = early[...]
    for s in range(STEPS):

        @pl.when(tab[T_IN + s] == 1)
        def _():
            final[tab[T_OWN + s]] = late[s]


def hidden_kernel(
    tab, tokens, early, rows, got, gain, w_q, q_gain, hidden, normed, query, all_scr, tok_scr, late
):
    total = got[0].astype(F32)
    for n in range(1, PARTS):
        total = total + got[n].astype(F32)
    late[...] = total
    for s in range(STEPS):
        at = slice(s * 8, s * 8 + 8)
        tok_scr[at, :] = tokens[s].astype(F32)
        all_scr[at, :] = tok_scr[at, :] + early[at, :]
    all_scr[OWN:, :] = rows[...] + total
    for s in range(STEPS):

        @pl.when(tab[T_IN + s] == 1)
        def _():
            for t in range(s, STEPS):
                at = pl.ds(t * 8 + tab[T_OWN + s], 1)
                row = LATE[s] + t - s
                all_scr[at, :] = tok_scr[at, :] + late[row : row + 1, :]

    total = all_scr[...]
    hidden[...] = total[:OWN]
    n2 = rms(total, gain[...].astype(F32)).astype(BF16)
    normed[...] = n2
    q = jnp.dot(n2[:OWN], w_q[...], preferred_element_type=F32)
    q = rms(q, q_gain[0:1, :].astype(F32)).astype(BF16)
    for n in range(PARTS):
        query[n] = q


def pages_kernel(place, table, tab, pages, got, query, kv, kv_gain, out, final, key, val, new, q_scr, o_scr):
    part = place[1]
    new[0] = rms(kv[0], kv_gain[1:2, :].astype(F32)).astype(BF16).astype(F32)
    new[1] = kv[1].astype(BF16).astype(F32)
    q_scr[...] = query[...].astype(F32)
    for i in range(64):
        page = table[i // 8, i % 8]
        key[i] = pages[page, 0].astype(F32)
        val[i] = pages[page, 1].astype(F32)

    def write(slot, length, row):
        offset = length & 63
        block = slot * 8 + lax.shift_right_logical(length, 6)

        @pl.when(lax.shift_right_logical(offset, 3) == part)
        def _():
            at = pl.ds(offset & 7, 1)
            key[block, at, :] = new[0, row : row + 1, :]
            val[block, at, :] = new[1, row : row + 1, :]

    column = lax.broadcasted_iota(jnp.int32, (1, 512), 1)
    column_slot = lax.shift_right_logical(column, 6)
    position = (lax.shift_right_logical(column, 3) & 7) * 64 + part * 8 + (column & 7)
    row_slot = lax.broadcasted_iota(jnp.int32, (64, 512), 0) & 7
    same = row_slot == lax.broadcasted_iota(jnp.int32, (64, 512), 1) // 64
    lane = lax.broadcasted_iota(jnp.int32, (64, 128), 1)
    for s in range(STEPS):
        slot = tab[T_OWN + s]

        @pl.when(tab[T_IN + s] == 1)
        def _():
            for i in range(INSTS):
                half = (i % 2) * 128
                rows = got[i].astype(F32)[32 + s * 8 : 40 + s * 8]
                to = key if (i // 2) % 2 == 0 else val
                to[slot * 8 + i // 4, :, half : half + 128] = rows
            for t in range(s):
                write(slot, tab[T_RLEN + FIRST[s] + t], OWN + FIRST[s] + t)

        lengths = jnp.zeros((1, 512), jnp.int32)
        for b in range(SLOTS):
            length = tab[T_OLEN + s * SLOTS + b]
            write(b, length, s * SLOTS + b)
            lengths = jnp.where(column_slot == b, length, lengths)
        visible = jnp.logical_and(same, position <= lengths)
        q = q_scr[:, s * 8 : s * 8 + 8, :].reshape(64, HD).astype(BF16)
        k = key[...].reshape(512, HD).astype(BF16)
        v = val[...].reshape(512, HD).astype(BF16)
        scores = lax.dot_general(
            q, k, (((1,), (1,)), ((), ())), preferred_element_type=F32
        ) * (float(HD) ** -0.5)
        scores = jnp.where(visible, scores, -1e30)
        top = jnp.max(scores, axis=-1, keepdims=True).astype(BF16).astype(F32)
        weights = jnp.where(visible, jnp.exp(scores - top), 0.0)
        total = jnp.sum(weights, axis=-1, keepdims=True)
        high = total.astype(BF16).astype(F32)
        low = total - high
        mixed = jnp.dot(weights.astype(BF16), v, preferred_element_type=F32)
        stats = jnp.where(lane == 0, top, jnp.where(lane == 1, high, jnp.where(lane == 2, low, 0.0)))
        mixed = jnp.concatenate([mixed, stats], axis=1)
        o_scr[:, s * 8 : s * 8 + 8, :] = mixed.reshape(PARTS, 8, 384)
    out[...] = o_scr[...].astype(BF16)
    for i in range(64):
        page = table[i // 8, i % 8]
        final[page, 0] = key[i].astype(BF16)
        final[page, 1] = val[i].astype(BF16)


def merge_kernel(got, w_o, out):
    shares = [got[n].astype(F32) for n in range(PARTS)]
    tops = [x[:, 256:257] for x in shares]
    top = tops[0]
    for x in tops[1:]:
        top = jnp.maximum(top, x)
    total = jnp.zeros((OWN, 1), F32)
    mixed = jnp.zeros((OWN, HD), F32)
    for x, own in zip(shares, tops, strict=True):
        scale = jnp.exp(own - top)
        total = total + (x[:, 257:258] + x[:, 258:259]) * scale
        mixed = mixed + x[:, :256] * scale
    head = (mixed / total).astype(BF16)
    part = jnp.dot(head, w_o[...], preferred_element_type=F32).astype(BF16)
    for n in range(PARTS):
        out[n] = part


def last_kernel(hidden, got, out):
    total = hidden[...]
    for n in range(PARTS):
        total = total + got[n].astype(F32)
    for s in range(STEPS):
        out[s] = total[s * 8 : s * 8 + 8].astype(BF16)


def body(
    step_tokens,
    delta_state,
    kv_pages,
    page_table,
    lengths,
    moves,
    delta_norm,
    head_norm,
    w_qk,
    w_vz,
    w_ba,
    a_log,
    dt_bias,
    w_out,
    att_norm,
    qk_norm,
    w_q,
    w_kv,
    w_o,
):
    shape = jax.ShapeDtypeStruct
    place = jnp.stack([lax.axis_index("inst"), lax.axis_index("tp")]).astype(jnp.int32)
    moves = moves.transpose(0, 2, 1)

    gain = delta_norm.reshape(1, D)
    heads = (a_log.reshape(1, 2), dt_bias.reshape(1, 2), head_norm.reshape(1, 128), w_out)

    def project(rows):
        return [
            jnp.einsum("bd,dtc->tbc", rows, w, preferred_element_type=F32)
            for w in (w_qk, w_vz, w_ba)
        ]

    (packed,) = call(
        pack_kernel,
        [SMEM, SMEM, SMEM, HBM, HBM, HBM],
        [shape((INSTS, PIECE, 128), BF16)],
        [
            pltpu.VMEM((STEPS, 2, 128, 128), F32),
            pltpu.VMEM((32, 2, 8, HD), BF16),
            pltpu.VMEM((STEPS, SLOTS, D), BF16),
            pltpu.VMEM((OWN, D), F32),
            pltpu.VMEM((8, D), F32),
            pltpu.SemaphoreType.DMA((37,)),
        ],
    )(moves, place, page_table, delta_state, kv_pages, step_tokens)
    got = lax.all_to_all(packed, "inst", 0, 0)

    (tab,) = call(
        table_kernel, [SMEM] * 3, [shape((T_SIZE,), jnp.int32)], out_specs=[SMEM]
    )(moves, place, lengths)
    (n1,) = call(
        norm_kernel, [VMEM] * 2, [shape((OWN, D), BF16)], [pltpu.VMEM((OWN, D), F32)]
    )(step_tokens, gain)
    rows_own = project(n1)
    early, early_state = call(
        early_kernel,
        [SMEM] + [VMEM] * 8,
        [shape((OWN, D), BF16), shape(delta_state.shape, F32)],
        [pltpu.VMEM((OWN, 256), F32)],
    )(tab, *rows_own, *heads, delta_state)

    (picked,) = call(
        select_kernel,
        [SMEM, VMEM, ANY],
        [shape((INSTS, PIECE, 128), BF16)],
        [pltpu.VMEM((INSTS * PIECE, 128), F32)] * 2,
    )(tab, got, early)
    got = lax.all_to_all(picked, "inst", 0, 0)

    for bit in (1, 2, 4):
        other = lax.ppermute(early, "tp", [(i, i ^ bit) for i in range(PARTS)])
        early = early.astype(F32) + other.astype(F32)
        if bit < 4:
            early = early.astype(BF16)

    n1, rows = call(
        late_norm_kernel,
        [VMEM] * 2,
        [shape((EXTRA, D), BF16), shape((EXTRA, D), F32)],
    )(got, gain)
    part, late_state = call(
        late_kernel,
        [SMEM] + [VMEM] * 11,
        [shape((PARTS, EXTRA, D), BF16), shape((STEPS, 2, 128, 128), F32)],
        [
            pltpu.VMEM((2, EXTRA, 128), F32),
            pltpu.VMEM((2, EXTRA, 256), F32),
            pltpu.VMEM((2, EXTRA, 2), F32),
            pltpu.VMEM((EXTRA, 256), F32),
        ],
    )(tab, *rows_own, *project(n1), *heads, got)
    parts = lax.all_to_all(part, "tp", 0, 0)
    (final_state,) = call(states_kernel, [SMEM, VMEM, VMEM], [shape(delta_state.shape, F32)])(
        tab, early_state, late_state
    )
    hidden, n2, query = call(
        hidden_kernel,
        [SMEM] + [VMEM] * 7,
        [shape((OWN, D), F32), shape((ROWS, D), BF16), shape((PARTS, OWN, HD), BF16)],
        [pltpu.VMEM((ROWS, D), F32), pltpu.VMEM((OWN, D), F32), pltpu.VMEM((EXTRA, D), F32)],
    )(tab, step_tokens, early, rows, parts, att_norm.reshape(1, D), w_q, qk_norm)
    queries = lax.all_to_all(query, "tp", 0, 0)
    kv = jnp.einsum("bd,dtc->tbc", n2, w_kv, preferred_element_type=F32)
    shares, final_pages = call(
        pages_kernel,
        [SMEM, SMEM, SMEM] + [VMEM] * 5,
        [shape((PARTS, OWN, 384), BF16), shape(kv_pages.shape, BF16)],
        [
            pltpu.VMEM((64, 8, HD), F32),
            pltpu.VMEM((64, 8, HD), F32),
            pltpu.VMEM((2, ROWS, HD), F32),
            pltpu.VMEM((PARTS, OWN, HD), F32),
            pltpu.VMEM((PARTS, OWN, 384), F32),
        ],
    )(place, page_table, tab, kv_pages, got, queries, kv, qk_norm)
    shares = lax.all_to_all(shares, "tp", 0, 0)
    (part,) = call(merge_kernel, [VMEM] * 2, [shape((PARTS, OWN, D), BF16)])(shares, w_o)
    parts = lax.all_to_all(part, "tp", 0, 0)
    (mixed,) = call(last_kernel, [VMEM] * 2, [shape(step_tokens.shape, BF16)])(hidden, parts)
    return (mixed, final_state, final_pages)


def solution(mesh):
    in_specs = (
        P(None, "inst", None),
        P("inst", "tp", None, None),
        P("inst", None, "tp", None),
        P("inst", None),
        P(),
        P(),
        P(),
        P(),
        P(None, None, "tp"),
        P(None, None, "tp"),
        P(None, None, "tp"),
        P("tp"),
        P("tp"),
        P("tp", None),
        P(),
        P(),
        P(None, "tp"),
        P(),
        P("tp", None),
    )
    out_specs = (P(None, "inst", None), P("inst", "tp", None, None), P("inst", None, "tp", None))
    return jax.shard_map(body, mesh=mesh, in_specs=in_specs, out_specs=out_specs, check_vma=False)
```

```python
import jax
import jax.numpy as jnp
from jax import lax
from jax.experimental import pallas as pl
from jax.experimental.pallas import tpu as pltpu
from jax.sharding import PartitionSpec as P

F32 = jnp.float32
BF16 = jnp.bfloat16
STEPS = 4
SLOTS = 8
INSTS = 32
PARTS = 8
OWN = 32
ROWS = 48
EXTRA = 16
PIECE = 72
DK = 128
HD = 256
D = 2048

T_SLOT = 0
T_FROM = 128
T_ITEM = 256
T_TOK = 384
T_OWN = 640
T_IN = 644
T_NEW = 648
T_RLEN = 656
T_OLEN = 664
T_SIZE = 768

FIRST = (0, 0, 1, 3)
LATE = (6, 10, 13, 15)

SMEM = pl.BlockSpec(memory_space=pltpu.SMEM)
VMEM = pl.BlockSpec()
ANY = pl.BlockSpec(memory_space=pl.ANY)


SOME, MOST = 16_000_000, 62_500_000
NEARLY = 62_000_000


def call(kernel, ins, outs, scratch=(), out_specs=None, vmem=SOME):
    return pl.pallas_call(
        kernel,
        in_specs=list(ins),
        out_specs=[VMEM] * len(outs) if out_specs is None else out_specs,
        out_shape=list(outs),
        scratch_shapes=list(scratch),
        compiler_params=pltpu.CompilerParams(vmem_limit_bytes=vmem),
    )


def rms(values, gain):
    return values * lax.rsqrt(jnp.mean(values * values, axis=-1, keepdims=True) + 1e-06) * gain


def unit(values):
    return values * lax.rsqrt(jnp.sum(values * values, axis=-1, keepdims=True) + 1e-06)


def own_slots(moves, me):
    slots = []
    for s in range(STEPS):
        slot = jnp.int32(0)
        for p in range(16):
            slot = jnp.where(moves[s, 0, p] == me, moves[s, 1, p], slot)
            slot = jnp.where(moves[s, 2, p] == me, moves[s, 3, p], slot)
        slots.append(slot)
    return slots


def pack_kernel(
    moves, table, state, pages, tokens, out, st_scr, pg_scr, bf_scr, tok_scr, row_scr, sem
):
    slots = own_slots(moves, lax.axis_index("inst"))
    token_copy = pltpu.make_async_copy(tokens, bf_scr, sem.at[36])
    token_copy.start()
    copies = []
    for s in range(STEPS):
        copies.append(pltpu.make_async_copy(state.at[slots[s]], st_scr.at[s], sem.at[32 + s]))
        for j in range(8):
            at = s * 8 + j
            copies.append(
                pltpu.make_async_copy(pages.at[table[slots[s], j]], pg_scr.at[at], sem.at[at])
            )
    for copy in copies:
        copy.start()
    token_copy.wait()
    for s in range(STEPS):
        tok_scr[s * 8 : s * 8 + 8, :] = bf_scr[s].astype(F32)
    row_scr[...] = jnp.zeros_like(row_scr)
    for s in range(STEPS):
        for t in range(s):
            row_scr[FIRST[s] + t : FIRST[s] + t + 1, :] = tok_scr[pl.ds(t * 8 + slots[s], 1), :]
    for copy in copies:
        copy.wait()
    blank = jnp.zeros((8, 128), F32)
    for i in range(INSTS):
        at, half = (i % 16) * 8, (i % 2) * 128
        tiles = [st_scr[s, i // 16, at : at + 8, :] for s in range(STEPS)]
        for s in range(STEPS):
            page = pg_scr[s * 8 + i // 4, (i // 2) % 2].astype(F32)
            tiles.append(page[:, half : half + 128])
        tiles.append(row_scr[:, i * 128 : i * 128 + 128] if i < 16 else blank)
        out[i] = jnp.concatenate(tiles, axis=0).astype(BF16)


def table_kernel(moves, place, lens, tab):
    for s in range(STEPS):
        for p in range(16):
            a, c, e, f = (moves[s, n, p] for n in range(4))
            source, target = a * SLOTS + c, e * SLOTS + f
            tab[T_SLOT + s * INSTS + a] = source
            tab[T_FROM + s * INSTS + a] = -1
            tab[T_SLOT + s * INSTS + e] = target
            tab[T_FROM + s * INSTS + e] = source
    me = place[0]

    def trace(e, s, at_row):
        cur = jnp.maximum(tab[T_FROM + s * INSTS + e], 0)
        hop = jnp.int32(s)
        fresh = {}
        for t in range(s - 1, -1, -1):
            h = lax.shift_right_logical(cur, 3)
            at_row(t, h, hop)
            slot, origin = tab[T_SLOT + t * INSTS + h], tab[T_FROM + t * INSTS + h]
            hit = slot == cur
            fresh[t] = jnp.logical_and(hit, origin < 0)
            moved = jnp.logical_and(hit, origin >= 0)
            cur = jnp.where(moved, origin, cur)
            hop = jnp.where(moved, t, hop)
        return cur, hop, fresh

    def route(e, carry):
        for s in range(STEPS):

            def at_row(t, h, hop, s=s):
                first = lax.shift_right_logical(hop * (hop - 1), 1)
                tab[T_TOK + e * 8 + FIRST[s] + t] = h * PIECE + 64 + first + t

            cur, hop, _ = trace(e, s, at_row)
            tab[T_ITEM + e * 4 + s] = lax.shift_right_logical(cur, 3) * PIECE + hop * 8
        return carry

    lax.fori_loop(0, INSTS, route, 0)

    held = [lens[me * SLOTS + b] for b in range(SLOTS)]
    for s in range(STEPS):
        slot = tab[T_SLOT + s * INSTS + me] & 7
        moved_in = tab[T_FROM + s * INSTS + me] >= 0
        tab[T_OWN + s] = slot
        tab[T_IN + s] = moved_in.astype(jnp.int32)
        root, _, fresh = trace(me, s, lambda t, h, hop: None)
        length = lens[root]
        for t in range(s):
            length = jnp.where(fresh[t], -t, length)
            tab[T_NEW + FIRST[s] + t] = fresh[t].astype(jnp.int32)
            tab[T_RLEN + FIRST[s] + t] = length + t
        arriving = jnp.where(moved_in, length, -s)
        for b in range(SLOTS):
            held[b] = jnp.where(slot == b, arriving, held[b])
            tab[T_OLEN + s * SLOTS + b] = held[b] + s


def select_kernel(tab, got, early, out, in_scr, out_scr):
    for h in range(INSTS):
        in_scr[h * PIECE : (h + 1) * PIECE, :] = got[h].astype(F32)
    for e in range(INSTS):
        out_scr[e * PIECE + 64 : (e + 1) * PIECE, :] = jnp.zeros((8, 128), F32)

    def pick(e, carry):
        base = e * PIECE
        for s in range(STEPS):
            item = tab[T_ITEM + e * 4 + s]
            for n in (0, 32):
                at = pl.ds(pl.multiple_of(item + n, 8), 8)
                to = pl.ds(pl.multiple_of(base + (s * 8 + n), 8), 8)
                out_scr[to, :] = in_scr[at, :]
        for r in range(6):
            out_scr[pl.ds(base + (64 + r), 1), :] = in_scr[pl.ds(tab[T_TOK + e * 8 + r], 1), :]
        return carry

    lax.fori_loop(0, INSTS, pick, 0, unroll=4)
    for e in range(INSTS):
        out[e] = out_scr[e * PIECE : (e + 1) * PIECE, :].astype(BF16)


def norm_kernel(tokens, gain, out, scr):
    for s in range(STEPS):
        scr[s * 8 : s * 8 + 8, :] = tokens[s].astype(F32)
    out[...] = rms(scr[...], gain[...].astype(F32)).astype(BF16)


def late_norm_kernel(got, gain, out, rows):
    rows[...] = jnp.zeros_like(rows)
    for i in range(16):
        rows[0:8, i * 128 : i * 128 + 128] = got[i].astype(F32)[64:]
    out[...] = rms(rows[...], gain[...].astype(F32)).astype(BF16)


def updater(qk, vz, ba, a_log, dt_bias, o_scr):
    rows = qk.shape[1]
    q = unit(qk[0]) * DK ** (-0.5)
    k = unit(qk[1])
    kq = jnp.broadcast_to(jnp.sum(k * q, axis=-1, keepdims=True), (rows, 128))
    q_cols, k_cols = q.T, k.T
    rate = jax.nn.sigmoid(ba[0])
    x = ba[1] + dt_bias[...]
    softplus = jnp.maximum(x, 0.0) + jnp.log1p(jnp.exp(-jnp.abs(x)))
    decay = jnp.exp(-jnp.exp(a_log[...]) * softplus)
    rates = [jnp.broadcast_to(rate[:, m : m + 1], (rows, 128)) for m in range(2)]
    decays = [jnp.broadcast_to(decay[:, m : m + 1], (rows, 128)) for m in range(2)]
    values = [vz[0, :, m * 128 : m * 128 + 128] for m in range(2)]

    def update(held, row, m):
        at = slice(row, row + 1)
        k_col, q_col = k_cols[:, at], q_cols[:, at]
        d = decays[m][at]
        u = rates[m][at] * (values[m][at] - d * jnp.sum(held * k_col, axis=0, keepdims=True))
        o = d * jnp.sum(held * q_col, axis=0, keepdims=True) + kq[at] * u
        o_scr[at, m * 128 : m * 128 + 128] = o
        return held * d + k_col * u

    return update


def gated(o_scr, z, gain, w_out):
    y = [
        rms(o_scr[:, m * 128 : m * 128 + 128], gain[...].astype(F32))
        * jax.nn.silu(z[:, m * 128 : m * 128 + 128])
        for m in range(2)
    ]
    y = jnp.concatenate(y, axis=1).astype(BF16)
    return jnp.dot(y, w_out[...], preferred_element_type=F32).astype(BF16)


def early_kernel(tab, qk, vz, ba, a_log, dt_bias, head_gain, w_out, state, out, final, o_scr):
    update = updater(qk, vz, ba, a_log, dt_bias, o_scr)
    final[...] = state[...]
    for s in range(STEPS):
        slot = tab[T_OWN + s]

        @pl.when(tab[T_IN + s] == 0)
        def _():
            final[slot] = jnp.zeros((2, 128, 128), F32)

        for b in range(SLOTS):
            for m in range(2):
                final[b, m] = update(final[b, m], s * SLOTS + b, m)
    out[...] = gated(o_scr, vz[1], head_gain, w_out)


def late_kernel(
    tab,
    qk,
    vz,
    ba,
    qk_in,
    vz_in,
    ba_in,
    a_log,
    dt_bias,
    head_gain,
    w_out,
    got,
    out,
    states,
    qk_scr,
    vz_scr,
    ba_scr,
    o_scr,
):
    for scr, new, old in ((qk_scr, qk_in, qk), (vz_scr, vz_in, vz), (ba_scr, ba_in, ba)):
        for n in range(2):
            scr[n, 0:8, :] = new[n, 0:8, :]
            for s in range(STEPS):
                for t in range(s, STEPS):
                    row = LATE[s] + t - s
                    scr[n, row : row + 1, :] = old[n, pl.ds(t * 8 + tab[T_OWN + s], 1), :]
    update = updater(qk_scr, vz_scr, ba_scr, a_log, dt_bias, o_scr)
    o_scr[...] = jnp.zeros_like(o_scr)
    for s in range(STEPS):
        slot = tab[T_OWN + s]

        @pl.when(tab[T_IN + s] == 1)
        def _():
            for m in range(2):
                held = jnp.concatenate(
                    [got[m * 16 + i].astype(F32)[s * 8 : s * 8 + 8] for i in range(16)], axis=0
                )
                for t in range(s):
                    r = FIRST[s] + t
                    held = jnp.where(tab[T_NEW + r] == 1, 0.0, held)
                    held = update(held, r, m)
                for t in range(s, STEPS):
                    if t > s:
                        leaves = jnp.logical_and(tab[T_OWN + t] == slot, tab[T_IN + t] == 0)
                        held = jnp.where(leaves, 0.0, held)
                    held = update(held, LATE[s] + t - s, m)
                states[s, m] = held

    part = gated(o_scr, vz_scr[1], head_gain, w_out)
    for n in range(PARTS):
        out[n] = part


def states_kernel(tab, early, late, final):
    final[...] = early[...]
    for s in range(STEPS):

        @pl.when(tab[T_IN + s] == 1)
        def _():
            final[tab[T_OWN + s]] = late[s]


def hidden_kernel(
    tab,
    done,
    tokens,
    early,
    rows,
    got,
    gain,
    w_q,
    q_gain,
    hidden,
    normed,
    query,
    all_scr,
    tok_scr,
    late,
):
    total = got[0].astype(F32)
    for n in range(1, PARTS):
        total = total + got[n].astype(F32)
    late[...] = total
    for s in range(STEPS):
        at = slice(s * 8, s * 8 + 8)
        tok_scr[at, :] = tokens[s].astype(F32)
        all_scr[at, :] = tok_scr[at, :] + early[at, :]
    all_scr[OWN:, :] = rows[...] + total
    for s in range(STEPS):

        @pl.when(tab[T_IN + s] == 1)
        def _():
            for t in range(s, STEPS):
                at = pl.ds(t * 8 + tab[T_OWN + s], 1)
                row = LATE[s] + t - s
                all_scr[at, :] = tok_scr[at, :] + late[row : row + 1, :]

    total = all_scr[...]
    hidden[...] = total[:OWN]
    n2 = rms(total, gain[...].astype(F32)).astype(BF16)
    normed[...] = n2
    q = jnp.dot(n2[:OWN], w_q[...], preferred_element_type=F32)
    q = rms(q, q_gain[0:1, :].astype(F32)).astype(BF16)
    for n in range(PARTS):
        query[n] = q


def pages_kernel(place, table, tab, pages, got, query, kv, kv_gain, out, final, key, val, new, q_scr, o_scr):
    part = place[1]
    new[0] = rms(kv[0], kv_gain[1:2, :].astype(F32)).astype(BF16).astype(F32)
    new[1] = kv[1].astype(BF16).astype(F32)
    q_scr[...] = query[...].astype(F32)
    for i in range(64):
        page = table[i // 8, i % 8]
        key[i] = pages[page, 0].astype(F32)
        val[i] = pages[page, 1].astype(F32)

    def write(slot, length, row):
        offset = length & 63
        block = slot * 8 + lax.shift_right_logical(length, 6)

        @pl.when(lax.shift_right_logical(offset, 3) == part)
        def _():
            at = pl.ds(offset & 7, 1)
            key[block, at, :] = new[0, row : row + 1, :]
            val[block, at, :] = new[1, row : row + 1, :]

    column = lax.broadcasted_iota(jnp.int32, (1, 512), 1)
    column_slot = lax.shift_right_logical(column, 6)
    position = (lax.shift_right_logical(column, 3) & 7) * 64 + part * 8 + (column & 7)
    row_slot = lax.broadcasted_iota(jnp.int32, (64, 512), 0) & 7
    same = row_slot == lax.broadcasted_iota(jnp.int32, (64, 512), 1) // 64
    lane = lax.broadcasted_iota(jnp.int32, (64, 128), 1)
    for s in range(STEPS):
        slot = tab[T_OWN + s]

        @pl.when(tab[T_IN + s] == 1)
        def _():
            for i in range(INSTS):
                half = (i % 2) * 128
                rows = got[i].astype(F32)[32 + s * 8 : 40 + s * 8]
                to = key if (i // 2) % 2 == 0 else val
                to[slot * 8 + i // 4, :, half : half + 128] = rows
            for t in range(s):
                write(slot, tab[T_RLEN + FIRST[s] + t], OWN + FIRST[s] + t)

        lengths = jnp.zeros((1, 512), jnp.int32)
        for b in range(SLOTS):
            length = tab[T_OLEN + s * SLOTS + b]
            write(b, length, s * SLOTS + b)
            lengths = jnp.where(column_slot == b, length, lengths)
        visible = jnp.logical_and(same, position <= lengths)
        q = q_scr[:, s * 8 : s * 8 + 8, :].reshape(64, HD).astype(BF16)
        k = key[...].reshape(512, HD).astype(BF16)
        v = val[...].reshape(512, HD).astype(BF16)
        scores = lax.dot_general(
            q, k, (((1,), (1,)), ((), ())), preferred_element_type=F32
        ) * (float(HD) ** -0.5)
        scores = jnp.where(visible, scores, -1e30)
        top = jnp.max(scores, axis=-1, keepdims=True).astype(BF16).astype(F32)
        weights = jnp.where(visible, jnp.exp(scores - top), 0.0)
        total = jnp.sum(weights, axis=-1, keepdims=True)
        high = total.astype(BF16).astype(F32)
        low = total - high
        mixed = jnp.dot(weights.astype(BF16), v, preferred_element_type=F32)
        stats = jnp.where(lane == 0, top, jnp.where(lane == 1, high, jnp.where(lane == 2, low, 0.0)))
        mixed = jnp.concatenate([mixed, stats], axis=1)
        o_scr[:, s * 8 : s * 8 + 8, :] = mixed.reshape(PARTS, 8, 384)
    out[...] = o_scr[...].astype(BF16)
    for i in range(64):
        page = table[i // 8, i % 8]
        final[page, 0] = key[i].astype(BF16)
        final[page, 1] = val[i].astype(BF16)


def merge_kernel(got, w_o, out):
    shares = [got[n].astype(F32) for n in range(PARTS)]
    tops = [x[:, 256:257] for x in shares]
    top = tops[0]
    for x in tops[1:]:
        top = jnp.maximum(top, x)
    total = jnp.zeros((OWN, 1), F32)
    mixed = jnp.zeros((OWN, HD), F32)
    for x, own in zip(shares, tops, strict=True):
        scale = jnp.exp(own - top)
        total = total + (x[:, 257:258] + x[:, 258:259]) * scale
        mixed = mixed + x[:, :256] * scale
    head = (mixed / total).astype(BF16)
    part = jnp.dot(head, w_o[...], preferred_element_type=F32).astype(BF16)
    for n in range(PARTS):
        out[n] = part


def last_kernel(hidden, got, out):
    total = hidden[...]
    for n in range(PARTS):
        total = total + got[n].astype(F32)
    for s in range(STEPS):
        out[s] = total[s * 8 : s * 8 + 8].astype(BF16)


def body(
    step_tokens,
    delta_state,
    kv_pages,
    page_table,
    lengths,
    moves,
    delta_norm,
    head_norm,
    w_qk,
    w_vz,
    w_ba,
    a_log,
    dt_bias,
    w_out,
    att_norm,
    qk_norm,
    w_q,
    w_kv,
    w_o,
):
    shape = jax.ShapeDtypeStruct
    place = jnp.stack([lax.axis_index("inst"), lax.axis_index("tp")]).astype(jnp.int32)
    moves = moves.transpose(0, 2, 1)

    gain = delta_norm.reshape(1, D)
    heads = (a_log.reshape(1, 2), dt_bias.reshape(1, 2), head_norm.reshape(1, 128), w_out)

    def project(rows):
        return [
            jnp.einsum("bd,dtc->tbc", rows, w, preferred_element_type=F32)
            for w in (w_qk, w_vz, w_ba)
        ]

    (packed,) = call(
        pack_kernel,
        [SMEM, SMEM, ANY, ANY, ANY],
        [shape((INSTS, PIECE, 128), BF16)],
        [
            pltpu.VMEM((STEPS, 2, 128, 128), F32),
            pltpu.VMEM((32, 2, 8, HD), BF16),
            pltpu.VMEM((STEPS, SLOTS, D), BF16),
            pltpu.VMEM((OWN, D), F32),
            pltpu.VMEM((8, D), F32),
            pltpu.SemaphoreType.DMA((37,)),
        ],
        vmem=MOST,
    )(moves, page_table, delta_state, kv_pages, step_tokens)
    got = lax.all_to_all(packed, "inst", 0, 0)

    (tab,) = call(
        table_kernel, [SMEM] * 3, [shape((T_SIZE,), jnp.int32)], out_specs=[SMEM]
    )(moves, place, lengths)
    (n1,) = call(
        norm_kernel, [VMEM] * 2, [shape((OWN, D), BF16)], [pltpu.VMEM((OWN, D), F32)]
    )(step_tokens, gain)
    rows_own = project(n1)
    early, early_state = call(
        early_kernel,
        [SMEM] + [VMEM] * 8,
        [shape((OWN, D), BF16), shape(delta_state.shape, F32)],
        [pltpu.VMEM((OWN, 256), F32)],
    )(tab, *rows_own, *heads, delta_state)

    (picked,) = call(
        select_kernel,
        [SMEM, VMEM, ANY],
        [shape((INSTS, PIECE, 128), BF16)],
        [pltpu.VMEM((INSTS * PIECE, 128), F32)] * 2,
    )(tab, got, early)
    got = lax.all_to_all(picked, "inst", 0, 0)

    for bit in (1, 2, 4):
        other = lax.ppermute(early, "tp", [(i, i ^ bit) for i in range(PARTS)])
        early = early.astype(F32) + other.astype(F32)
        if bit < 4:
            early = early.astype(BF16)

    n1, rows = call(
        late_norm_kernel,
        [VMEM] * 2,
        [shape((EXTRA, D), BF16), shape((EXTRA, D), F32)],
    )(got, gain)
    part, late_state = call(
        late_kernel,
        [SMEM] + [VMEM] * 11,
        [shape((PARTS, EXTRA, D), BF16), shape((STEPS, 2, 128, 128), F32)],
        [
            pltpu.VMEM((2, EXTRA, 128), F32),
            pltpu.VMEM((2, EXTRA, 256), F32),
            pltpu.VMEM((2, EXTRA, 2), F32),
            pltpu.VMEM((EXTRA, 256), F32),
        ],
    )(tab, *rows_own, *project(n1), *heads, got)
    parts = lax.all_to_all(part, "tp", 0, 0)
    (final_state,) = call(states_kernel, [SMEM, VMEM, VMEM], [shape(delta_state.shape, F32)])(
        tab, early_state, late_state
    )
    hidden, n2, query = call(
        hidden_kernel,
        [SMEM, ANY] + [VMEM] * 7,
        [shape((OWN, D), F32), shape((ROWS, D), BF16), shape((PARTS, OWN, HD), BF16)],
        [pltpu.VMEM((ROWS, D), F32), pltpu.VMEM((OWN, D), F32), pltpu.VMEM((EXTRA, D), F32)],
        vmem=NEARLY,
    )(tab, final_state, step_tokens, early, rows, parts, att_norm.reshape(1, D), w_q, qk_norm)
    queries = lax.all_to_all(query, "tp", 0, 0)
    kv = jnp.einsum("bd,dtc->tbc", n2, w_kv, preferred_element_type=F32)
    shares, final_pages = call(
        pages_kernel,
        [SMEM, SMEM, SMEM] + [VMEM] * 5,
        [shape((PARTS, OWN, 384), BF16), shape(kv_pages.shape, BF16)],
        [
            pltpu.VMEM((64, 8, HD), F32),
            pltpu.VMEM((64, 8, HD), F32),
            pltpu.VMEM((2, ROWS, HD), F32),
            pltpu.VMEM((PARTS, OWN, HD), F32),
            pltpu.VMEM((PARTS, OWN, 384), F32),
        ],
    )(place, page_table, tab, kv_pages, got, queries, kv, qk_norm)
    shares = lax.all_to_all(shares, "tp", 0, 0)
    (part,) = call(merge_kernel, [VMEM] * 2, [shape((PARTS, OWN, D), BF16)])(shares, w_o)
    parts = lax.all_to_all(part, "tp", 0, 0)
    (mixed,) = call(last_kernel, [VMEM] * 2, [shape(step_tokens.shape, BF16)])(hidden, parts)
    return (mixed, final_state, final_pages)


def solution(mesh):
    in_specs = (
        P(None, "inst", None),
        P("inst", "tp", None, None),
        P("inst", None, "tp", None),
        P("inst", None),
        P(),
        P(),
        P(),
        P(),
        P(None, None, "tp"),
        P(None, None, "tp"),
        P(None, None, "tp"),
        P("tp"),
        P("tp"),
        P("tp", None),
        P(),
        P(),
        P(None, "tp"),
        P(),
        P("tp", None),
    )
    out_specs = (P(None, "inst", None), P("inst", "tp", None, None), P("inst", None, "tp", None))
    return jax.shard_map(body, mesh=mesh, in_specs=in_specs, out_specs=out_specs, check_vma=False)
```

```python
import jax
import jax.numpy as jnp
from jax import lax
from jax.experimental import pallas as pl
from jax.experimental.pallas import tpu as pltpu
from jax.sharding import PartitionSpec as P

F32 = jnp.float32
BF16 = jnp.bfloat16
STEPS = 4
SLOTS = 8
INSTS = 32
PARTS = 8
OWN = 32
ROWS = 48
EXTRA = 16
PIECE = 72
DK = 128
HD = 256
D = 2048

T_SLOT = 0
T_FROM = 128
T_ITEM = 256
T_TOK = 384
T_OWN = 640
T_IN = 644
T_NEW = 648
T_RLEN = 656
T_OLEN = 664
T_SIZE = 768

FIRST = (0, 0, 1, 3)
LATE = (6, 10, 13, 15)

SMEM = pl.BlockSpec(memory_space=pltpu.SMEM)
VMEM = pl.BlockSpec()
ANY = pl.BlockSpec(memory_space=pl.ANY)


SOME, MOST = 16_000_000, 62_500_000
NEARLY = 62_000_000


def call(kernel, ins, outs, scratch=(), out_specs=None, vmem=SOME):
    return pl.pallas_call(
        kernel,
        in_specs=list(ins),
        out_specs=[VMEM] * len(outs) if out_specs is None else out_specs,
        out_shape=list(outs),
        scratch_shapes=list(scratch),
        compiler_params=pltpu.CompilerParams(vmem_limit_bytes=vmem),
    )


def rms(values, gain):
    return values * lax.rsqrt(jnp.mean(values * values, axis=-1, keepdims=True) + 1e-06) * gain


def unit(values):
    return values * lax.rsqrt(jnp.sum(values * values, axis=-1, keepdims=True) + 1e-06)


def own_slots(moves, me):
    slots = []
    for s in range(STEPS):
        slot = jnp.int32(0)
        for p in range(16):
            slot = jnp.where(moves[s, 0, p] == me, moves[s, 1, p], slot)
            slot = jnp.where(moves[s, 2, p] == me, moves[s, 3, p], slot)
        slots.append(slot)
    return slots


def pack_kernel(
    moves, table, state, pages, tokens, out, st_scr, pg_scr, bf_scr, tok_scr, row_scr, sem
):
    slots = own_slots(moves, lax.axis_index("inst"))
    token_copy = pltpu.make_async_copy(tokens, bf_scr, sem.at[36])
    token_copy.start()
    copies = []
    for s in range(STEPS):
        copies.append(pltpu.make_async_copy(state.at[slots[s]], st_scr.at[s], sem.at[32 + s]))
        for j in range(8):
            at = s * 8 + j
            copies.append(
                pltpu.make_async_copy(pages.at[table[slots[s], j]], pg_scr.at[at], sem.at[at])
            )
    for copy in copies:
        copy.start()
    token_copy.wait()
    for s in range(STEPS):
        tok_scr[s * 8 : s * 8 + 8, :] = bf_scr[s].astype(F32)
    row_scr[...] = jnp.zeros_like(row_scr)
    for s in range(STEPS):
        for t in range(s):
            row_scr[FIRST[s] + t : FIRST[s] + t + 1, :] = tok_scr[pl.ds(t * 8 + slots[s], 1), :]
    for copy in copies:
        copy.wait()
    blank = jnp.zeros((8, 128), F32)
    for i in range(INSTS):
        at, half = (i % 16) * 8, (i % 2) * 128
        tiles = [st_scr[s, i // 16, at : at + 8, :] for s in range(STEPS)]
        for s in range(STEPS):
            page = pg_scr[s * 8 + i // 4, (i // 2) % 2].astype(F32)
            tiles.append(page[:, half : half + 128])
        tiles.append(row_scr[:, i * 128 : i * 128 + 128] if i < 16 else blank)
        out[i] = jnp.concatenate(tiles, axis=0).astype(BF16)


def table_kernel(moves, place, lens, tab):
    for s in range(STEPS):
        for p in range(16):
            a, c, e, f = (moves[s, n, p] for n in range(4))
            source, target = a * SLOTS + c, e * SLOTS + f
            tab[T_SLOT + s * INSTS + a] = source
            tab[T_FROM + s * INSTS + a] = -1
            tab[T_SLOT + s * INSTS + e] = target
            tab[T_FROM + s * INSTS + e] = source
    me = place[0]

    def trace(e, s, at_row):
        cur = jnp.maximum(tab[T_FROM + s * INSTS + e], 0)
        hop = jnp.int32(s)
        fresh = {}
        for t in range(s - 1, -1, -1):
            h = lax.shift_right_logical(cur, 3)
            at_row(t, h, hop)
            slot, origin = tab[T_SLOT + t * INSTS + h], tab[T_FROM + t * INSTS + h]
            hit = slot == cur
            fresh[t] = jnp.logical_and(hit, origin < 0)
            moved = jnp.logical_and(hit, origin >= 0)
            cur = jnp.where(moved, origin, cur)
            hop = jnp.where(moved, t, hop)
        return cur, hop, fresh

    def route(e, carry):
        for s in range(STEPS):

            def at_row(t, h, hop, s=s):
                first = lax.shift_right_logical(hop * (hop - 1), 1)
                tab[T_TOK + e * 8 + FIRST[s] + t] = h * PIECE + 64 + first + t

            cur, hop, _ = trace(e, s, at_row)
            tab[T_ITEM + e * 4 + s] = lax.shift_right_logical(cur, 3) * PIECE + hop * 8
        return carry

    lax.fori_loop(0, INSTS, route, 0)

    held = [lens[me * SLOTS + b] for b in range(SLOTS)]
    for s in range(STEPS):
        slot = tab[T_SLOT + s * INSTS + me] & 7
        moved_in = tab[T_FROM + s * INSTS + me] >= 0
        tab[T_OWN + s] = slot
        tab[T_IN + s] = moved_in.astype(jnp.int32)
        root, _, fresh = trace(me, s, lambda t, h, hop: None)
        length = lens[root]
        for t in range(s):
            length = jnp.where(fresh[t], -t, length)
            tab[T_NEW + FIRST[s] + t] = fresh[t].astype(jnp.int32)
            tab[T_RLEN + FIRST[s] + t] = length + t
        arriving = jnp.where(moved_in, length, -s)
        for b in range(SLOTS):
            held[b] = jnp.where(slot == b, arriving, held[b])
            tab[T_OLEN + s * SLOTS + b] = held[b] + s


def select_kernel(tab, got, early, out, in_scr, out_scr):
    for h in range(INSTS):
        in_scr[h * PIECE : (h + 1) * PIECE, :] = got[h].astype(F32)
    for e in range(INSTS):
        out_scr[e * PIECE + 64 : (e + 1) * PIECE, :] = jnp.zeros((8, 128), F32)

    def pick(e, carry):
        base = e * PIECE
        for s in range(STEPS):
            item = tab[T_ITEM + e * 4 + s]
            for n in (0, 32):
                at = pl.ds(pl.multiple_of(item + n, 8), 8)
                to = pl.ds(pl.multiple_of(base + (s * 8 + n), 8), 8)
                out_scr[to, :] = in_scr[at, :]
        for r in range(6):
            out_scr[pl.ds(base + (64 + r), 1), :] = in_scr[pl.ds(tab[T_TOK + e * 8 + r], 1), :]
        return carry

    lax.fori_loop(0, INSTS, pick, 0, unroll=4)
    for e in range(INSTS):
        out[e] = out_scr[e * PIECE : (e + 1) * PIECE, :].astype(BF16)


def norm_kernel(tokens, gain, out, scr):
    for s in range(STEPS):
        scr[s * 8 : s * 8 + 8, :] = tokens[s].astype(F32)
    out[...] = rms(scr[...], gain[...].astype(F32)).astype(BF16)


def late_norm_kernel(got, gain, out, rows):
    rows[...] = jnp.zeros_like(rows)
    for i in range(16):
        rows[0:8, i * 128 : i * 128 + 128] = got[i].astype(F32)[64:]
    out[...] = rms(rows[...], gain[...].astype(F32)).astype(BF16)


def updater(qk, vz, ba, a_log, dt_bias, o_scr):
    rows = qk.shape[1]
    q = unit(qk[0]) * DK ** (-0.5)
    k = unit(qk[1])
    kq = jnp.broadcast_to(jnp.sum(k * q, axis=-1, keepdims=True), (rows, 128))
    q_cols, k_cols = q.T, k.T
    rate = jax.nn.sigmoid(ba[0])
    x = ba[1] + dt_bias[...]
    softplus = jnp.maximum(x, 0.0) + jnp.log1p(jnp.exp(-jnp.abs(x)))
    decay = jnp.exp(-jnp.exp(a_log[...]) * softplus)
    rates = [jnp.broadcast_to(rate[:, m : m + 1], (rows, 128)) for m in range(2)]
    decays = [jnp.broadcast_to(decay[:, m : m + 1], (rows, 128)) for m in range(2)]
    values = [vz[0, :, m * 128 : m * 128 + 128] for m in range(2)]

    def update(held, row, m):
        at = slice(row, row + 1)
        k_col, q_col = k_cols[:, at], q_cols[:, at]
        d = decays[m][at]
        u = rates[m][at] * (values[m][at] - d * jnp.sum(held * k_col, axis=0, keepdims=True))
        o = d * jnp.sum(held * q_col, axis=0, keepdims=True) + kq[at] * u
        o_scr[at, m * 128 : m * 128 + 128] = o
        return held * d + k_col * u

    return update


def gated(o_scr, z, gain, w_out):
    y = [
        rms(o_scr[:, m * 128 : m * 128 + 128], gain[...].astype(F32))
        * jax.nn.silu(z[:, m * 128 : m * 128 + 128])
        for m in range(2)
    ]
    y = jnp.concatenate(y, axis=1).astype(BF16)
    return jnp.dot(y, w_out[...], preferred_element_type=F32).astype(BF16)


def early_kernel(tab, qk, vz, ba, a_log, dt_bias, head_gain, w_out, state, out, final, o_scr):
    update = updater(qk, vz, ba, a_log, dt_bias, o_scr)
    final[...] = state[...]
    for s in range(STEPS):
        slot = tab[T_OWN + s]

        @pl.when(tab[T_IN + s] == 0)
        def _():
            final[slot] = jnp.zeros((2, 128, 128), F32)

        for b in range(SLOTS):
            for m in range(2):
                final[b, m] = update(final[b, m], s * SLOTS + b, m)
    out[...] = gated(o_scr, vz[1], head_gain, w_out)


def late_kernel(
    tab,
    qk,
    vz,
    ba,
    qk_in,
    vz_in,
    ba_in,
    a_log,
    dt_bias,
    head_gain,
    w_out,
    got,
    out,
    states,
    qk_scr,
    vz_scr,
    ba_scr,
    o_scr,
):
    for scr, new, old in ((qk_scr, qk_in, qk), (vz_scr, vz_in, vz), (ba_scr, ba_in, ba)):
        for n in range(2):
            scr[n, 0:8, :] = new[n, 0:8, :]
            for s in range(STEPS):
                for t in range(s, STEPS):
                    row = LATE[s] + t - s
                    scr[n, row : row + 1, :] = old[n, pl.ds(t * 8 + tab[T_OWN + s], 1), :]
    update = updater(qk_scr, vz_scr, ba_scr, a_log, dt_bias, o_scr)
    o_scr[...] = jnp.zeros_like(o_scr)
    for s in range(STEPS):
        slot = tab[T_OWN + s]

        @pl.when(tab[T_IN + s] == 1)
        def _():
            for m in range(2):
                held = jnp.concatenate(
                    [got[m * 16 + i].astype(F32)[s * 8 : s * 8 + 8] for i in range(16)], axis=0
                )
                for t in range(s):
                    r = FIRST[s] + t
                    held = jnp.where(tab[T_NEW + r] == 1, 0.0, held)
                    held = update(held, r, m)
                for t in range(s, STEPS):
                    if t > s:
                        leaves = jnp.logical_and(tab[T_OWN + t] == slot, tab[T_IN + t] == 0)
                        held = jnp.where(leaves, 0.0, held)
                    held = update(held, LATE[s] + t - s, m)
                states[s, m] = held

    part = gated(o_scr, vz_scr[1], head_gain, w_out)
    for n in range(PARTS):
        out[n] = part


def states_kernel(tab, early, late, final):
    final[...] = early[...]
    for s in range(STEPS):

        @pl.when(tab[T_IN + s] == 1)
        def _():
            final[tab[T_OWN + s]] = late[s]


def hidden_kernel(
    tab,
    done,
    tokens,
    early,
    rows,
    got,
    gain,
    w_q,
    q_gain,
    hidden,
    normed,
    query,
    all_scr,
    tok_scr,
    late,
):
    total = got[0].astype(F32)
    for n in range(1, PARTS):
        total = total + got[n].astype(F32)
    late[...] = total
    for s in range(STEPS):
        at = slice(s * 8, s * 8 + 8)
        tok_scr[at, :] = tokens[s].astype(F32)
        all_scr[at, :] = tok_scr[at, :] + early[at, :]
    all_scr[OWN:, :] = rows[...] + total
    for s in range(STEPS):

        @pl.when(tab[T_IN + s] == 1)
        def _():
            for t in range(s, STEPS):
                at = pl.ds(t * 8 + tab[T_OWN + s], 1)
                row = LATE[s] + t - s
                all_scr[at, :] = tok_scr[at, :] + late[row : row + 1, :]

    total = all_scr[...]
    hidden[...] = total[:OWN]
    n2 = rms(total, gain[...].astype(F32)).astype(BF16)
    normed[...] = n2
    q = jnp.dot(n2[:OWN], w_q[...], preferred_element_type=F32)
    q = rms(q, q_gain[0:1, :].astype(F32)).astype(BF16)
    for n in range(PARTS):
        query[n] = q


def pages_kernel(place, table, tab, pages, got, query, kv, kv_gain, out, final, key, val, new, q_scr, o_scr):
    part = place[1]
    new[0] = rms(kv[0], kv_gain[1:2, :].astype(F32)).astype(BF16).astype(F32)
    new[1] = kv[1].astype(BF16).astype(F32)
    q_scr[...] = query[...].astype(F32)
    for i in range(64):
        page = table[i // 8, i % 8]
        key[i] = pages[page, 0].astype(F32)
        val[i] = pages[page, 1].astype(F32)

    def write(slot, length, row):
        offset = length & 63
        block = slot * 8 + lax.shift_right_logical(length, 6)
        block = jnp.where(lax.shift_right_logical(offset, 3) == part, block, 64)
        at = pl.ds(offset & 7, 1)
        key[block, at, :] = new[0, row : row + 1, :]
        val[block, at, :] = new[1, row : row + 1, :]

    column = lax.broadcasted_iota(jnp.int32, (1, 512), 1)
    column_slot = lax.shift_right_logical(column, 6)
    position = (lax.shift_right_logical(column, 3) & 7) * 64 + part * 8 + (column & 7)
    row_slot = lax.broadcasted_iota(jnp.int32, (64, 512), 0) & 7
    same = row_slot == lax.broadcasted_iota(jnp.int32, (64, 512), 1) // 64
    lane = lax.broadcasted_iota(jnp.int32, (64, 128), 1)
    for s in range(STEPS):
        slot = tab[T_OWN + s]

        @pl.when(tab[T_IN + s] == 1)
        def _():
            for i in range(INSTS):
                half = (i % 2) * 128
                rows = got[i].astype(F32)[32 + s * 8 : 40 + s * 8]
                to = key if (i // 2) % 2 == 0 else val
                to[slot * 8 + i // 4, :, half : half + 128] = rows
            for t in range(s):
                write(slot, tab[T_RLEN + FIRST[s] + t], OWN + FIRST[s] + t)

        lengths = jnp.zeros((1, 512), jnp.int32)
        for b in range(SLOTS):
            length = tab[T_OLEN + s * SLOTS + b]
            write(b, length, s * SLOTS + b)
            lengths = jnp.where(column_slot == b, length, lengths)
        visible = jnp.logical_and(same, position <= lengths)
        q = q_scr[:, s * 8 : s * 8 + 8, :].reshape(64, HD).astype(BF16)
        k = key[:64].reshape(512, HD).astype(BF16)
        v = val[:64].reshape(512, HD).astype(BF16)
        scores = lax.dot_general(
            q, k, (((1,), (1,)), ((), ())), preferred_element_type=F32
        ) * (float(HD) ** -0.5)
        scores = jnp.where(visible, scores, -1e30)
        top = jnp.max(scores, axis=-1, keepdims=True).astype(BF16).astype(F32)
        weights = jnp.where(visible, jnp.exp(scores - top), 0.0)
        total = jnp.sum(weights, axis=-1, keepdims=True)
        high = total.astype(BF16).astype(F32)
        low = total - high
        mixed = jnp.dot(weights.astype(BF16), v, preferred_element_type=F32)
        stats = jnp.where(lane == 0, top, jnp.where(lane == 1, high, jnp.where(lane == 2, low, 0.0)))
        mixed = jnp.concatenate([mixed, stats], axis=1)
        o_scr[:, s * 8 : s * 8 + 8, :] = mixed.reshape(PARTS, 8, 384)
    out[...] = o_scr[...].astype(BF16)
    for i in range(64):
        page = table[i // 8, i % 8]
        final[page, 0] = key[i].astype(BF16)
        final[page, 1] = val[i].astype(BF16)


def merge_kernel(got, w_o, out):
    shares = [got[n].astype(F32) for n in range(PARTS)]
    tops = [x[:, 256:257] for x in shares]
    top = tops[0]
    for x in tops[1:]:
        top = jnp.maximum(top, x)
    total = jnp.zeros((OWN, 1), F32)
    mixed = jnp.zeros((OWN, HD), F32)
    for x, own in zip(shares, tops, strict=True):
        scale = jnp.exp(own - top)
        total = total + (x[:, 257:258] + x[:, 258:259]) * scale
        mixed = mixed + x[:, :256] * scale
    head = (mixed / total).astype(BF16)
    part = jnp.dot(head, w_o[...], preferred_element_type=F32).astype(BF16)
    for n in range(PARTS):
        out[n] = part


def last_kernel(hidden, got, out):
    total = hidden[...]
    for n in range(PARTS):
        total = total + got[n].astype(F32)
    for s in range(STEPS):
        out[s] = total[s * 8 : s * 8 + 8].astype(BF16)


def body(
    step_tokens,
    delta_state,
    kv_pages,
    page_table,
    lengths,
    moves,
    delta_norm,
    head_norm,
    w_qk,
    w_vz,
    w_ba,
    a_log,
    dt_bias,
    w_out,
    att_norm,
    qk_norm,
    w_q,
    w_kv,
    w_o,
):
    shape = jax.ShapeDtypeStruct
    place = jnp.stack([lax.axis_index("inst"), lax.axis_index("tp")]).astype(jnp.int32)
    moves = moves.transpose(0, 2, 1)

    gain = delta_norm.reshape(1, D)
    heads = (a_log.reshape(1, 2), dt_bias.reshape(1, 2), head_norm.reshape(1, 128), w_out)

    def project(rows):
        return [
            jnp.einsum("bd,dtc->tbc", rows, w, preferred_element_type=F32)
            for w in (w_qk, w_vz, w_ba)
        ]

    (packed,) = call(
        pack_kernel,
        [SMEM, SMEM, ANY, ANY, ANY],
        [shape((INSTS, PIECE, 128), BF16)],
        [
            pltpu.VMEM((STEPS, 2, 128, 128), F32),
            pltpu.VMEM((32, 2, 8, HD), BF16),
            pltpu.VMEM((STEPS, SLOTS, D), BF16),
            pltpu.VMEM((OWN, D), F32),
            pltpu.VMEM((8, D), F32),
            pltpu.SemaphoreType.DMA((37,)),
        ],
        vmem=MOST,
    )(moves, page_table, delta_state, kv_pages, step_tokens)
    got = lax.all_to_all(packed, "inst", 0, 0)

    (tab,) = call(
        table_kernel, [SMEM] * 3, [shape((T_SIZE,), jnp.int32)], out_specs=[SMEM]
    )(moves, place, lengths)
    (n1,) = call(
        norm_kernel, [VMEM] * 2, [shape((OWN, D), BF16)], [pltpu.VMEM((OWN, D), F32)]
    )(step_tokens, gain)
    rows_own = project(n1)
    early, early_state = call(
        early_kernel,
        [SMEM] + [VMEM] * 8,
        [shape((OWN, D), BF16), shape(delta_state.shape, F32)],
        [pltpu.VMEM((OWN, 256), F32)],
    )(tab, *rows_own, *heads, delta_state)

    (picked,) = call(
        select_kernel,
        [SMEM, VMEM, ANY],
        [shape((INSTS, PIECE, 128), BF16)],
        [pltpu.VMEM((INSTS * PIECE, 128), F32)] * 2,
    )(tab, got, early)
    got = lax.all_to_all(picked, "inst", 0, 0)

    for bit in (1, 2, 4):
        other = lax.ppermute(early, "tp", [(i, i ^ bit) for i in range(PARTS)])
        early = early.astype(F32) + other.astype(F32)
        if bit < 4:
            early = early.astype(BF16)

    n1, rows = call(
        late_norm_kernel,
        [VMEM] * 2,
        [shape((EXTRA, D), BF16), shape((EXTRA, D), F32)],
    )(got, gain)
    part, late_state = call(
        late_kernel,
        [SMEM] + [VMEM] * 11,
        [shape((PARTS, EXTRA, D), BF16), shape((STEPS, 2, 128, 128), F32)],
        [
            pltpu.VMEM((2, EXTRA, 128), F32),
            pltpu.VMEM((2, EXTRA, 256), F32),
            pltpu.VMEM((2, EXTRA, 2), F32),
            pltpu.VMEM((EXTRA, 256), F32),
        ],
    )(tab, *rows_own, *project(n1), *heads, got)
    parts = lax.all_to_all(part, "tp", 0, 0)
    (final_state,) = call(states_kernel, [SMEM, VMEM, VMEM], [shape(delta_state.shape, F32)])(
        tab, early_state, late_state
    )
    hidden, n2, query = call(
        hidden_kernel,
        [SMEM, ANY] + [VMEM] * 7,
        [shape((OWN, D), F32), shape((ROWS, D), BF16), shape((PARTS, OWN, HD), BF16)],
        [pltpu.VMEM((ROWS, D), F32), pltpu.VMEM((OWN, D), F32), pltpu.VMEM((EXTRA, D), F32)],
        vmem=NEARLY,
    )(tab, final_state, step_tokens, early, rows, parts, att_norm.reshape(1, D), w_q, qk_norm)
    queries = lax.all_to_all(query, "tp", 0, 0)
    kv = jnp.einsum("bd,dtc->tbc", n2, w_kv, preferred_element_type=F32)
    shares, final_pages = call(
        pages_kernel,
        [SMEM, SMEM, SMEM] + [VMEM] * 5,
        [shape((PARTS, OWN, 384), BF16), shape(kv_pages.shape, BF16)],
        [
            pltpu.VMEM((65, 8, HD), F32),
            pltpu.VMEM((65, 8, HD), F32),
            pltpu.VMEM((2, ROWS, HD), F32),
            pltpu.VMEM((PARTS, OWN, HD), F32),
            pltpu.VMEM((PARTS, OWN, 384), F32),
        ],
    )(place, page_table, tab, kv_pages, got, queries, kv, qk_norm)
    shares = lax.all_to_all(shares, "tp", 0, 0)
    (part,) = call(merge_kernel, [VMEM] * 2, [shape((PARTS, OWN, D), BF16)])(shares, w_o)
    parts = lax.all_to_all(part, "tp", 0, 0)
    (mixed,) = call(last_kernel, [VMEM] * 2, [shape(step_tokens.shape, BF16)])(hidden, parts)
    return (mixed, final_state, final_pages)


def solution(mesh):
    in_specs = (
        P(None, "inst", None),
        P("inst", "tp", None, None),
        P("inst", None, "tp", None),
        P("inst", None),
        P(),
        P(),
        P(),
        P(),
        P(None, None, "tp"),
        P(None, None, "tp"),
        P(None, None, "tp"),
        P("tp"),
        P("tp"),
        P("tp", None),
        P(),
        P(),
        P(None, "tp"),
        P(),
        P("tp", None),
    )
    out_specs = (P(None, "inst", None), P("inst", "tp", None, None), P("inst", None, "tp", None))
    return jax.shard_map(body, mesh=mesh, in_specs=in_specs, out_specs=out_specs, check_vma=False)
```

```python
import jax
import jax.numpy as jnp
from jax import lax
from jax.experimental import pallas as pl
from jax.experimental.pallas import tpu as pltpu
from jax.sharding import PartitionSpec as P

F32 = jnp.float32
BF16 = jnp.bfloat16
STEPS = 4
SLOTS = 8
INSTS = 32
PARTS = 8
OWN = 32
ROWS = 48
EXTRA = 16
PIECE = 72
DK = 128
HD = 256
D = 2048

T_SLOT = 0
T_FROM = 128
T_ITEM = 256
T_TOK = 384
T_OWN = 640
T_IN = 644
T_NEW = 648
T_RLEN = 656
T_OLEN = 664
T_SIZE = 768

FIRST = (0, 0, 1, 3)
LATE = (6, 10, 13, 15)

SMEM = pl.BlockSpec(memory_space=pltpu.SMEM)
VMEM = pl.BlockSpec()
ANY = pl.BlockSpec(memory_space=pl.ANY)


SOME, MOST = 16_000_000, 62_500_000
NEARLY = 62_000_000


def call(kernel, ins, outs, scratch=(), out_specs=None, vmem=SOME):
    return pl.pallas_call(
        kernel,
        in_specs=list(ins),
        out_specs=[VMEM] * len(outs) if out_specs is None else out_specs,
        out_shape=list(outs),
        scratch_shapes=list(scratch),
        compiler_params=pltpu.CompilerParams(vmem_limit_bytes=vmem),
    )


def rms(values, gain):
    return values * lax.rsqrt(jnp.mean(values * values, axis=-1, keepdims=True) + 1e-06) * gain


def unit(values):
    return values * lax.rsqrt(jnp.sum(values * values, axis=-1, keepdims=True) + 1e-06)


def own_slot(moves, me, s):
    slot = jnp.int32(0)
    for p in range(16):
        slot = jnp.where(moves[s, 0, p] == me, moves[s, 1, p], slot)
        slot = jnp.where(moves[s, 2, p] == me, moves[s, 3, p], slot)
    return slot


def pack_kernel(
    moves, table, state, pages, tokens, out, st_scr, pg_scr, bf_scr, tok_scr, row_scr, sem
):
    token_copy = pltpu.make_async_copy(tokens, bf_scr, sem.at[36])
    token_copy.start()
    me = lax.axis_index("inst")
    copies, slots = [], []
    for s in range(STEPS):
        slots.append(own_slot(moves, me, s))
        copies.append(pltpu.make_async_copy(state.at[slots[s]], st_scr.at[s], sem.at[32 + s]))
        for j in range(8):
            at = s * 8 + j
            copies.append(
                pltpu.make_async_copy(pages.at[table[slots[s], j]], pg_scr.at[at], sem.at[at])
            )
        for copy in copies[s * 9 :]:
            copy.start()
    token_copy.wait()
    for s in range(STEPS):
        tok_scr[s * 8 : s * 8 + 8, :] = bf_scr[s].astype(F32)
    row_scr[...] = jnp.zeros_like(row_scr)
    for s in range(STEPS):
        for t in range(s):
            row_scr[FIRST[s] + t : FIRST[s] + t + 1, :] = tok_scr[pl.ds(t * 8 + slots[s], 1), :]
    for copy in copies:
        copy.wait()
    blank = jnp.zeros((8, 128), F32)
    for i in range(INSTS):
        at, half = (i % 16) * 8, (i % 2) * 128
        tiles = [st_scr[s, i // 16, at : at + 8, :] for s in range(STEPS)]
        for s in range(STEPS):
            page = pg_scr[s * 8 + i // 4, (i // 2) % 2].astype(F32)
            tiles.append(page[:, half : half + 128])
        tiles.append(row_scr[:, i * 128 : i * 128 + 128] if i < 16 else blank)
        out[i] = jnp.concatenate(tiles, axis=0).astype(BF16)


def table_kernel(moves, place, lens, tab):
    for s in range(STEPS):
        for p in range(16):
            a, c, e, f = (moves[s, n, p] for n in range(4))
            source, target = a * SLOTS + c, e * SLOTS + f
            tab[T_SLOT + s * INSTS + a] = source
            tab[T_FROM + s * INSTS + a] = -1
            tab[T_SLOT + s * INSTS + e] = target
            tab[T_FROM + s * INSTS + e] = source
    me = place[0]

    def trace(e, s, at_row):
        cur = jnp.maximum(tab[T_FROM + s * INSTS + e], 0)
        hop = jnp.int32(s)
        fresh = {}
        for t in range(s - 1, -1, -1):
            h = lax.shift_right_logical(cur, 3)
            at_row(t, h, hop)
            slot, origin = tab[T_SLOT + t * INSTS + h], tab[T_FROM + t * INSTS + h]
            hit = slot == cur
            fresh[t] = jnp.logical_and(hit, origin < 0)
            moved = jnp.logical_and(hit, origin >= 0)
            cur = jnp.where(moved, origin, cur)
            hop = jnp.where(moved, t, hop)
        return cur, hop, fresh

    def route(e, carry):
        for s in range(STEPS):

            def at_row(t, h, hop, s=s):
                first = lax.shift_right_logical(hop * (hop - 1), 1)
                tab[T_TOK + e * 8 + FIRST[s] + t] = h * PIECE + 64 + first + t

            cur, hop, _ = trace(e, s, at_row)
            tab[T_ITEM + e * 4 + s] = lax.shift_right_logical(cur, 3) * PIECE + hop * 8
        return carry

    lax.fori_loop(0, INSTS, route, 0)

    held = [lens[me * SLOTS + b] for b in range(SLOTS)]
    for s in range(STEPS):
        slot = tab[T_SLOT + s * INSTS + me] & 7
        moved_in = tab[T_FROM + s * INSTS + me] >= 0
        tab[T_OWN + s] = slot
        tab[T_IN + s] = moved_in.astype(jnp.int32)
        root, _, fresh = trace(me, s, lambda t, h, hop: None)
        length = lens[root]
        for t in range(s):
            length = jnp.where(fresh[t], -t, length)
            tab[T_NEW + FIRST[s] + t] = fresh[t].astype(jnp.int32)
            tab[T_RLEN + FIRST[s] + t] = length + t
        arriving = jnp.where(moved_in, length, -s)
        for b in range(SLOTS):
            held[b] = jnp.where(slot == b, arriving, held[b])
            tab[T_OLEN + s * SLOTS + b] = held[b] + s


def select_kernel(tab, got, early, out, in_scr, out_scr):
    for h in range(INSTS):
        in_scr[h * PIECE : (h + 1) * PIECE, :] = got[h].astype(F32)
    for e in range(INSTS):
        out_scr[e * PIECE + 64 : (e + 1) * PIECE, :] = jnp.zeros((8, 128), F32)

    def pick(e, carry):
        base = e * PIECE
        for s in range(STEPS):
            item = tab[T_ITEM + e * 4 + s]
            for n in (0, 32):
                at = pl.ds(pl.multiple_of(item + n, 8), 8)
                to = pl.ds(pl.multiple_of(base + (s * 8 + n), 8), 8)
                out_scr[to, :] = in_scr[at, :]
        for r in range(6):
            out_scr[pl.ds(base + (64 + r), 1), :] = in_scr[pl.ds(tab[T_TOK + e * 8 + r], 1), :]
        return carry

    lax.fori_loop(0, INSTS, pick, 0, unroll=4)
    for e in range(INSTS):
        out[e] = out_scr[e * PIECE : (e + 1) * PIECE, :].astype(BF16)


def norm_kernel(tokens, gain, out, scr):
    for s in range(STEPS):
        scr[s * 8 : s * 8 + 8, :] = tokens[s].astype(F32)
    out[...] = rms(scr[...], gain[...].astype(F32)).astype(BF16)


def late_norm_kernel(got, gain, out, rows):
    rows[...] = jnp.zeros_like(rows)
    for i in range(16):
        rows[0:8, i * 128 : i * 128 + 128] = got[i].astype(F32)[64:]
    out[...] = rms(rows[...], gain[...].astype(F32)).astype(BF16)


def updater(qk, vz, ba, a_log, dt_bias, o_scr):
    rows = qk.shape[1]
    q = unit(qk[0]) * DK ** (-0.5)
    k = unit(qk[1])
    kq = jnp.broadcast_to(jnp.sum(k * q, axis=-1, keepdims=True), (rows, 128))
    q_cols, k_cols = q.T, k.T
    rate = jax.nn.sigmoid(ba[0])
    x = ba[1] + dt_bias[...]
    softplus = jnp.maximum(x, 0.0) + jnp.log1p(jnp.exp(-jnp.abs(x)))
    decay = jnp.exp(-jnp.exp(a_log[...]) * softplus)
    rates = [jnp.broadcast_to(rate[:, m : m + 1], (rows, 128)) for m in range(2)]
    decays = [jnp.broadcast_to(decay[:, m : m + 1], (rows, 128)) for m in range(2)]
    values = [vz[0, :, m * 128 : m * 128 + 128] for m in range(2)]

    def update(held, row, m):
        at = slice(row, row + 1)
        k_col, q_col = k_cols[:, at], q_cols[:, at]
        d = decays[m][at]
        u = rates[m][at] * (values[m][at] - d * jnp.sum(held * k_col, axis=0, keepdims=True))
        o = d * jnp.sum(held * q_col, axis=0, keepdims=True) + kq[at] * u
        o_scr[at, m * 128 : m * 128 + 128] = o
        return held * d + k_col * u

    return update


def gated(o_scr, z, gain, w_out):
    y = [
        rms(o_scr[:, m * 128 : m * 128 + 128], gain[...].astype(F32))
        * jax.nn.silu(z[:, m * 128 : m * 128 + 128])
        for m in range(2)
    ]
    y = jnp.concatenate(y, axis=1).astype(BF16)
    return jnp.dot(y, w_out[...], preferred_element_type=F32).astype(BF16)


def early_kernel(tab, qk, vz, ba, a_log, dt_bias, head_gain, w_out, state, out, final, o_scr):
    update = updater(qk, vz, ba, a_log, dt_bias, o_scr)
    final[...] = state[...]
    for s in range(STEPS):
        slot = tab[T_OWN + s]

        @pl.when(tab[T_IN + s] == 0)
        def _():
            final[slot] = jnp.zeros((2, 128, 128), F32)

        for b in range(SLOTS):
            for m in range(2):
                final[b, m] = update(final[b, m], s * SLOTS + b, m)
    out[...] = gated(o_scr, vz[1], head_gain, w_out)


def late_kernel(
    tab,
    qk,
    vz,
    ba,
    qk_in,
    vz_in,
    ba_in,
    a_log,
    dt_bias,
    head_gain,
    w_out,
    got,
    out,
    states,
    qk_scr,
    vz_scr,
    ba_scr,
    o_scr,
):
    for scr, new, old in ((qk_scr, qk_in, qk), (vz_scr, vz_in, vz), (ba_scr, ba_in, ba)):
        for n in range(2):
            scr[n, 0:8, :] = new[n, 0:8, :]
            for s in range(STEPS):
                for t in range(s, STEPS):
                    row = LATE[s] + t - s
                    scr[n, row : row + 1, :] = old[n, pl.ds(t * 8 + tab[T_OWN + s], 1), :]
    update = updater(qk_scr, vz_scr, ba_scr, a_log, dt_bias, o_scr)
    o_scr[...] = jnp.zeros_like(o_scr)
    for s in range(STEPS):
        slot = tab[T_OWN + s]

        @pl.when(tab[T_IN + s] == 1)
        def _():
            for m in range(2):
                held = jnp.concatenate(
                    [got[m * 16 + i].astype(F32)[s * 8 : s * 8 + 8] for i in range(16)], axis=0
                )
                for t in range(s):
                    r = FIRST[s] + t
                    held = jnp.where(tab[T_NEW + r] == 1, 0.0, held)
                    held = update(held, r, m)
                for t in range(s, STEPS):
                    if t > s:
                        leaves = jnp.logical_and(tab[T_OWN + t] == slot, tab[T_IN + t] == 0)
                        held = jnp.where(leaves, 0.0, held)
                    held = update(held, LATE[s] + t - s, m)
                states[s, m] = held

    part = gated(o_scr, vz_scr[1], head_gain, w_out)
    for n in range(PARTS):
        out[n] = part


def states_kernel(tab, early, late, final):
    final[...] = early[...]
    for s in range(STEPS):

        @pl.when(tab[T_IN + s] == 1)
        def _():
            final[tab[T_OWN + s]] = late[s]


def hidden_kernel(
    tab,
    done,
    tokens,
    early,
    rows,
    got,
    gain,
    w_q,
    q_gain,
    hidden,
    normed,
    query,
    all_scr,
    tok_scr,
    late,
):
    total = got[0].astype(F32)
    for n in range(1, PARTS):
        total = total + got[n].astype(F32)
    late[...] = total
    for s in range(STEPS):
        at = slice(s * 8, s * 8 + 8)
        tok_scr[at, :] = tokens[s].astype(F32)
        all_scr[at, :] = tok_scr[at, :] + early[at, :]
    all_scr[OWN:, :] = rows[...] + total
    for s in range(STEPS):

        @pl.when(tab[T_IN + s] == 1)
        def _():
            for t in range(s, STEPS):
                at = pl.ds(t * 8 + tab[T_OWN + s], 1)
                row = LATE[s] + t - s
                all_scr[at, :] = tok_scr[at, :] + late[row : row + 1, :]

    total = all_scr[...]
    hidden[...] = total[:OWN]
    n2 = rms(total, gain[...].astype(F32)).astype(BF16)
    normed[...] = n2
    q = jnp.dot(n2[:OWN], w_q[...], preferred_element_type=F32)
    q = rms(q, q_gain[0:1, :].astype(F32)).astype(BF16)
    for n in range(PARTS):
        query[n] = q


def pages_kernel(place, table, tab, pages, got, query, kv, kv_gain, out, final, key, val, new, q_scr, o_scr):
    part = place[1]
    new[0] = rms(kv[0], kv_gain[1:2, :].astype(F32)).astype(BF16).astype(F32)
    new[1] = kv[1].astype(BF16).astype(F32)
    q_scr[...] = query[...].astype(F32)
    for i in range(64):
        page = table[i // 8, i % 8]
        key[i] = pages[page, 0].astype(F32)
        val[i] = pages[page, 1].astype(F32)

    def write(slot, length, row):
        offset = length & 63
        block = slot * 8 + lax.shift_right_logical(length, 6)
        block = jnp.where(lax.shift_right_logical(offset, 3) == part, block, 64)
        at = pl.ds(offset & 7, 1)
        key[block, at, :] = new[0, row : row + 1, :]
        val[block, at, :] = new[1, row : row + 1, :]

    column = lax.broadcasted_iota(jnp.int32, (1, 512), 1)
    column_slot = lax.shift_right_logical(column, 6)
    position = (lax.shift_right_logical(column, 3) & 7) * 64 + part * 8 + (column & 7)
    row_slot = lax.broadcasted_iota(jnp.int32, (64, 512), 0) & 7
    same = row_slot == lax.broadcasted_iota(jnp.int32, (64, 512), 1) // 64
    lane = lax.broadcasted_iota(jnp.int32, (64, 128), 1)
    for s in range(STEPS):
        slot = tab[T_OWN + s]

        @pl.when(tab[T_IN + s] == 1)
        def _():
            for i in range(INSTS):
                half = (i % 2) * 128
                rows = got[i].astype(F32)[32 + s * 8 : 40 + s * 8]
                to = key if (i // 2) % 2 == 0 else val
                to[slot * 8 + i // 4, :, half : half + 128] = rows
            for t in range(s):
                write(slot, tab[T_RLEN + FIRST[s] + t], OWN + FIRST[s] + t)

        lengths = jnp.zeros((1, 512), jnp.int32)
        for b in range(SLOTS):
            length = tab[T_OLEN + s * SLOTS + b]
            write(b, length, s * SLOTS + b)
            lengths = jnp.where(column_slot == b, length, lengths)
        visible = jnp.logical_and(same, position <= lengths)
        q = q_scr[:, s * 8 : s * 8 + 8, :].reshape(64, HD).astype(BF16)
        k = key[:64].reshape(512, HD).astype(BF16)
        v = val[:64].reshape(512, HD).astype(BF16)
        scores = lax.dot_general(
            q, k, (((1,), (1,)), ((), ())), preferred_element_type=F32
        ) * (float(HD) ** -0.5)
        scores = jnp.where(visible, scores, -1e30)
        top = jnp.max(scores, axis=-1, keepdims=True).astype(BF16).astype(F32)
        weights = jnp.where(visible, jnp.exp(scores - top), 0.0)
        total = jnp.sum(weights, axis=-1, keepdims=True)
        high = total.astype(BF16).astype(F32)
        low = total - high
        mixed = jnp.dot(weights.astype(BF16), v, preferred_element_type=F32)
        stats = jnp.where(lane == 0, top, jnp.where(lane == 1, high, jnp.where(lane == 2, low, 0.0)))
        mixed = jnp.concatenate([mixed, stats], axis=1)
        o_scr[:, s * 8 : s * 8 + 8, :] = mixed.reshape(PARTS, 8, 384)
    out[...] = o_scr[...].astype(BF16)
    for i in range(64):
        page = table[i // 8, i % 8]
        final[page, 0] = key[i].astype(BF16)
        final[page, 1] = val[i].astype(BF16)


def merge_kernel(got, w_o, out):
    shares = [got[n].astype(F32) for n in range(PARTS)]
    tops = [x[:, 256:257] for x in shares]
    top = tops[0]
    for x in tops[1:]:
        top = jnp.maximum(top, x)
    total = jnp.zeros((OWN, 1), F32)
    mixed = jnp.zeros((OWN, HD), F32)
    for x, own in zip(shares, tops, strict=True):
        scale = jnp.exp(own - top)
        total = total + (x[:, 257:258] + x[:, 258:259]) * scale
        mixed = mixed + x[:, :256] * scale
    head = (mixed / total).astype(BF16)
    part = jnp.dot(head, w_o[...], preferred_element_type=F32).astype(BF16)
    for n in range(PARTS):
        out[n] = part


def last_kernel(hidden, got, out):
    total = hidden[...]
    for n in range(PARTS):
        total = total + got[n].astype(F32)
    for s in range(STEPS):
        out[s] = total[s * 8 : s * 8 + 8].astype(BF16)


def body(
    step_tokens,
    delta_state,
    kv_pages,
    page_table,
    lengths,
    moves,
    delta_norm,
    head_norm,
    w_qk,
    w_vz,
    w_ba,
    a_log,
    dt_bias,
    w_out,
    att_norm,
    qk_norm,
    w_q,
    w_kv,
    w_o,
):
    shape = jax.ShapeDtypeStruct
    place = jnp.stack([lax.axis_index("inst"), lax.axis_index("tp")]).astype(jnp.int32)
    moves = moves.transpose(0, 2, 1)

    gain = delta_norm.reshape(1, D)
    heads = (a_log.reshape(1, 2), dt_bias.reshape(1, 2), head_norm.reshape(1, 128), w_out)

    def project(rows):
        return [
            jnp.einsum("bd,dtc->tbc", rows, w, preferred_element_type=F32)
            for w in (w_qk, w_vz, w_ba)
        ]

    (packed,) = call(
        pack_kernel,
        [SMEM, SMEM, ANY, ANY, ANY],
        [shape((INSTS, PIECE, 128), BF16)],
        [
            pltpu.VMEM((STEPS, 2, 128, 128), F32),
            pltpu.VMEM((32, 2, 8, HD), BF16),
            pltpu.VMEM((STEPS, SLOTS, D), BF16),
            pltpu.VMEM((OWN, D), F32),
            pltpu.VMEM((8, D), F32),
            pltpu.SemaphoreType.DMA((37,)),
        ],
        vmem=MOST,
    )(moves, page_table, delta_state, kv_pages, step_tokens)
    got = lax.all_to_all(packed, "inst", 0, 0)

    (tab,) = call(
        table_kernel, [SMEM] * 3, [shape((T_SIZE,), jnp.int32)], out_specs=[SMEM]
    )(moves, place, lengths)
    (n1,) = call(
        norm_kernel, [VMEM] * 2, [shape((OWN, D), BF16)], [pltpu.VMEM((OWN, D), F32)]
    )(step_tokens, gain)
    rows_own = project(n1)
    early, early_state = call(
        early_kernel,
        [SMEM] + [VMEM] * 8,
        [shape((OWN, D), BF16), shape(delta_state.shape, F32)],
        [pltpu.VMEM((OWN, 256), F32)],
    )(tab, *rows_own, *heads, delta_state)

    (picked,) = call(
        select_kernel,
        [SMEM, VMEM, ANY],
        [shape((INSTS, PIECE, 128), BF16)],
        [pltpu.VMEM((INSTS * PIECE, 128), F32)] * 2,
    )(tab, got, early)
    got = lax.all_to_all(picked, "inst", 0, 0)

    for bit in (1, 2, 4):
        other = lax.ppermute(early, "tp", [(i, i ^ bit) for i in range(PARTS)])
        early = early.astype(F32) + other.astype(F32)
        if bit < 4:
            early = early.astype(BF16)

    n1, rows = call(
        late_norm_kernel,
        [VMEM] * 2,
        [shape((EXTRA, D), BF16), shape((EXTRA, D), F32)],
    )(got, gain)
    part, late_state = call(
        late_kernel,
        [SMEM] + [VMEM] * 11,
        [shape((PARTS, EXTRA, D), BF16), shape((STEPS, 2, 128, 128), F32)],
        [
            pltpu.VMEM((2, EXTRA, 128), F32),
            pltpu.VMEM((2, EXTRA, 256), F32),
            pltpu.VMEM((2, EXTRA, 2), F32),
            pltpu.VMEM((EXTRA, 256), F32),
        ],
    )(tab, *rows_own, *project(n1), *heads, got)
    parts = lax.all_to_all(part, "tp", 0, 0)
    (final_state,) = call(states_kernel, [SMEM, VMEM, VMEM], [shape(delta_state.shape, F32)])(
        tab, early_state, late_state
    )
    hidden, n2, query = call(
        hidden_kernel,
        [SMEM, ANY] + [VMEM] * 7,
        [shape((OWN, D), F32), shape((ROWS, D), BF16), shape((PARTS, OWN, HD), BF16)],
        [pltpu.VMEM((ROWS, D), F32), pltpu.VMEM((OWN, D), F32), pltpu.VMEM((EXTRA, D), F32)],
        vmem=NEARLY,
    )(tab, final_state, step_tokens, early, rows, parts, att_norm.reshape(1, D), w_q, qk_norm)
    queries = lax.all_to_all(query, "tp", 0, 0)
    kv = jnp.einsum("bd,dtc->tbc", n2, w_kv, preferred_element_type=F32)
    shares, final_pages = call(
        pages_kernel,
        [SMEM, SMEM, SMEM] + [VMEM] * 5,
        [shape((PARTS, OWN, 384), BF16), shape(kv_pages.shape, BF16)],
        [
            pltpu.VMEM((65, 8, HD), F32),
            pltpu.VMEM((65, 8, HD), F32),
            pltpu.VMEM((2, ROWS, HD), F32),
            pltpu.VMEM((PARTS, OWN, HD), F32),
            pltpu.VMEM((PARTS, OWN, 384), F32),
        ],
    )(place, page_table, tab, kv_pages, got, queries, kv, qk_norm)
    shares = lax.all_to_all(shares, "tp", 0, 0)
    (part,) = call(merge_kernel, [VMEM] * 2, [shape((PARTS, OWN, D), BF16)])(shares, w_o)
    parts = lax.all_to_all(part, "tp", 0, 0)
    (mixed,) = call(last_kernel, [VMEM] * 2, [shape(step_tokens.shape, BF16)])(hidden, parts)
    return (mixed, final_state, final_pages)


def solution(mesh):
    in_specs = (
        P(None, "inst", None),
        P("inst", "tp", None, None),
        P("inst", None, "tp", None),
        P("inst", None),
        P(),
        P(),
        P(),
        P(),
        P(None, None, "tp"),
        P(None, None, "tp"),
        P(None, None, "tp"),
        P("tp"),
        P("tp"),
        P("tp", None),
        P(),
        P(),
        P(None, "tp"),
        P(),
        P("tp", None),
    )
    out_specs = (P(None, "inst", None), P("inst", "tp", None, None), P("inst", None, "tp", None))
    return jax.shard_map(body, mesh=mesh, in_specs=in_specs, out_specs=out_specs, check_vma=False)
```
